512 devices in a mesh: section: 8 (over y, core), chan: 16 (over z), rep: 4 (over x).
Axes of the slice: x: 4, y: 4, z: 16, core: 2. Of those that a mesh axis runs over, the one named last changes fastest.
Arguments:
- latent: bfloat16 [8, 1280, 64], P('rep', 'chan'), parts along dimension 0, may hold values from -6 to 6
- stale_rows: bfloat16 [4, 8, 8, 1280, 2, 32], P(None, 'section', 'rep', 'chan'), parts along dimension 2, may hold values from -5 to 5
- conv_weight: bfloat16 [8, 9, 1280, 1280], P('section', None, 'chan'), may hold values from -0.078125 to 0.078125
- conv_bias: float32 [8, 1280], P('section', 'chan'), may hold values from -1.5 to 1.5
- norm_gain: float32 [8, 1280], P('section', 'chan'), may hold values from 0.5 to 1.5
- norm_shift: float32 [8, 1280], P('section', 'chan'), may hold values from -2.5 to 2.5
- time_proj: bfloat16 [8, 320, 1280], P('section', None, 'chan'), may hold values from -0.3125 to 0.3125
- patch_order: int32 [2], replicated, may hold values from 0 to 1, each once
- timestep: int32 [4], P('rep'), parts along dimension 0, may hold values from 0 to 999
- stale_step: int32 [8, 2], P('section'), may hold values from 0 to 3
Outputs:
- segment_out: bfloat16 [8, 8, 1280, 64], P('section', 'rep', 'chan'), parts along dimension 1
The draws below stay inside these ranges and needn't reach their ends.
There are 4 independent parts, one for each index of `rep`. The reference program is written for one: setup_inputs(seed, part) draws one part's arguments, and reference() takes and returns one part's arrays. A program takes and returns all parts, laid end to end along the dimension named above; an argument that names none is the same for every part. Nothing has to cross between parts.
Inputs may be any that keep to these rules, and one draw needn't show every extreme that they name: `patch_order`: each patch appears once.
All inputs are finite; a program needn't handle non-finite values.
Results may differ from the reference program's by a relative error of at most 0.017.
Values may be sent and summed in bfloat16 or wider, within the bound.
A program may use at most 64 MiB of HBM per device.

```python
import math
import jax
import jax.numpy as jnp
from jax import lax

C = 1280
GROUPS = 32
TDIM = 320
PATCHES = 2
HP = 2
W = 32
STALE = 4
SECTIONS = 8


def set_ends(entries, key, low, high):
    extent = entries.shape
    spot = [jax.random.randint(jax.random.fold_in(key, axis), (), 0, extent[axis]) for axis in range(len(extent))]
    entries = entries.at[tuple(spot)].set(low)
    longest = extent.index(max(extent))
    spot[longest] = (spot[longest] + 1) % extent[longest]
    return entries.at[tuple(spot)].set(high)


def spiked(array, rng, source, target, blocks, factor):
    owner, partner = [(jnp.arange(array.shape[position]) // (array.shape[position] // blocks)).reshape([-1 if axis == position else 1 for axis in range(array.ndim)]) for position in (source, target)]
    chosen = jax.random.permutation(rng, blocks)[partner]
    strong = (owner == chosen) | (owner == (partner + blocks // 2) % blocks)
    return jnp.where(strong, factor * array, array)


def block_levels(own_key, shape, pieces, smallest, high):
    def one(position, shards_of):
        steps = jax.random.uniform(jax.random.fold_in(jax.random.fold_in(own_key, 6), position), (shards_of,), jnp.float32, smallest / len(pieces), high / len(pieces))
        return jnp.repeat(jnp.exp(steps), shape[position] // shards_of).reshape((-1,) + (1,) * (len(shape) - position - 1))

    factor_of = one(*pieces[0])
    for cut in pieces[1:]:
        factor_of = factor_of * one(*cut)
    return factor_of


def scatter_about(key, shape, spread, most, pieces=(), held_as=jnp.bfloat16):
    loudness = block_levels(key, shape, pieces, -0.22, 0.18) if pieces else 1.0
    drawn = jax.random.normal(key, shape, jnp.float32) * spread * loudness
    return jnp.minimum(jnp.maximum(drawn, -most), most).astype(held_as)


def bell_draw_with(own_key, shape, scale, reach, pieces, heavy, held_as=jnp.bfloat16):
    values = scale * jax.random.normal(own_key, shape, jnp.float32)
    if pieces:
        values = values * block_levels(own_key, shape, pieces, -0.22, 0.18)
    return jnp.clip(spiked(values, jax.random.fold_in(own_key, 3), *heavy), -reach, reach).astype(held_as)


def setup_inputs(seed: int = 0, part: int = 0) -> dict:
    keys = jax.random.split(jax.random.key(seed), 11)
    own_keys = jax.random.split(jax.random.fold_in(keys[10], part), 11)
    latent = scatter_about(own_keys[0], (PATCHES, C, HP * W), 1.0, 6.0, ((1, 16),))
    stale_rows = scatter_about(own_keys[1], (STALE, SECTIONS, PATCHES, C, 2, W), 0.7, 5.0, ((1, 8), (3, 16)))
    conv_weight = bell_draw_with(keys[2], (SECTIONS, 9, C, C), (9 * C) ** -0.5, 0.078125, ((0, 8), (2, 16)), (2, 3, 16, 2.0))
    conv_bias = scatter_about(keys[3], (SECTIONS, C), 0.3, 1.5, ((0, 8), (1, 16)), jnp.float32)
    norm_gain = jnp.clip(0.5 + 1.0 * jax.random.uniform(keys[4], (SECTIONS, C), jnp.float32) ** block_levels(keys[4], (SECTIONS, C), ((0, 8), (1, 16)), -0.2, 0.2), 0.5, 1.5)
    norm_shift = scatter_about(keys[5], (SECTIONS, C), 0.5, 2.5, ((0, 8), (1, 16)), jnp.float32)
    time_proj = scatter_about(keys[6], (SECTIONS, TDIM, C), TDIM ** -0.5, 0.3125, ((0, 8), (2, 16)))
    patch_order = jax.random.permutation(keys[7], PATCHES).astype(jnp.int32)
    timestep = jax.random.randint(own_keys[8], (1,), 0, 1000).astype(jnp.int32)
    stale_step = set_ends(jax.random.randint(keys[9], (SECTIONS, PATCHES), 0, STALE), jax.random.fold_in(keys[9], 1), 0, STALE - 1).astype(jnp.int32)
    return dict(latent=latent, stale_rows=stale_rows, conv_weight=conv_weight, conv_bias=conv_bias, norm_gain=norm_gain, norm_shift=norm_shift, time_proj=time_proj, patch_order=patch_order, timestep=timestep, stale_step=stale_step)


def pick_bank(stale_rows, stale_step):
    levels = jnp.arange(stale_rows.shape[0], dtype=jnp.int32)
    chosen = (stale_step.astype(jnp.int32)[None, :, :] == levels[:, None, None])[:, :, :, None, None, None]
    picked = jnp.where(chosen, stale_rows.astype(jnp.float32), jnp.float32(0.0))
    return lax.optimization_barrier(jnp.sum(picked, axis=0)).astype(jnp.bfloat16)

def reference(latent, stale_rows, conv_weight, conv_bias, norm_gain, norm_shift, time_proj, patch_order, timestep, stale_step):
    cells = HP * W
    index = jnp.arange(PATCHES, dtype=jnp.int32)
    rank = lax.optimization_barrier(jnp.sum(jnp.where(patch_order[:, None] == index[None, :], index[:, None], 0), axis=0)).astype(jnp.int32)
    half = TDIM // 2
    freqs = jnp.exp(-math.log(10000.0) * jnp.arange(half, dtype=jnp.float32) / half)
    angles = timestep.astype(jnp.float32)[0] * freqs
    emb = jnp.concatenate([jnp.cos(angles), jnp.sin(angles)])
    semb = jax.nn.silu(emb).astype(jnp.bfloat16)[None, :]
    bank = pick_bank(stale_rows, stale_step)
    rank_up = jnp.concatenate([rank[:1], rank[:-1]])
    rank_down = jnp.concatenate([rank[1:], rank[-1:]])
    fresh_top = (rank_up < rank)[:, None, None]
    fresh_bottom = (rank_down < rank)[:, None, None]
    zero_row = jnp.zeros((1, C, W), jnp.bfloat16)
    state = latent
    outputs = []
    for s in range(SECTIONS):
        xf = state.astype(jnp.float32)
        grouped = xf.reshape(PATCHES, GROUPS, -1)
        mean = lax.optimization_barrier(jnp.mean(grouped, axis=2, keepdims=True))
        var = lax.optimization_barrier(jnp.mean((grouped - mean) ** 2, axis=2, keepdims=True))
        normed = ((grouped - mean) / jnp.sqrt(var + 1e-05)).reshape(PATCHES, C, cells)
        normed = normed * norm_gain[s][None, :, None] + norm_shift[s][None, :, None]
        hidden = jax.nn.silu(normed).astype(jnp.bfloat16).reshape(PATCHES, C, HP, W)
        top_new = jnp.concatenate([zero_row, hidden[:-1, :, HP - 1, :]], axis=0)
        top_old = jnp.concatenate([zero_row, bank[s, :-1, :, 1, :]], axis=0)
        top = jnp.where(fresh_top, top_new, top_old)
        bottom_new = jnp.concatenate([hidden[1:, :, 0, :], zero_row], axis=0)
        bottom_old = jnp.concatenate([bank[s, 1:, :, 0, :], zero_row], axis=0)
        bottom = jnp.where(fresh_bottom, bottom_new, bottom_old)
        extended = jnp.concatenate([top[:, :, None, :], hidden, bottom[:, :, None, :]], axis=2)
        extended = jnp.pad(extended, ((0, 0), (0, 0), (0, 0), (1, 1)))
        taps = jnp.stack([extended[:, :, a:a + HP, b:b + W] for a in range(3) for b in range(3)], axis=0)
        taps = jnp.transpose(taps, (0, 2, 1, 3, 4)).reshape(9 * C, PATCHES * cells)
        weights = conv_weight[s].reshape(9 * C, C)
        conv = jnp.dot(weights.T, taps, preferred_element_type=jnp.float32)
        conv = jnp.transpose(conv.reshape(C, PATCHES, cells), (1, 0, 2))
        temb = jnp.dot(semb, time_proj[s], preferred_element_type=jnp.float32)[0]
        result = (xf + conv + conv_bias[s][None, :, None] + temb[None, :, None]).astype(jnp.bfloat16)
        outputs.append(result)
        state = result
    return jnp.stack(outputs)
```

```python
import functools
import math

import jax
import jax.numpy as jnp
from jax import lax
from jax.experimental import pallas as pl
from jax.experimental.pallas import tpu as pltpu
from jax.sharding import PartitionSpec as P

C = 1280
TDIM = 320
W = 32
CELLS = 64
STALE = 4
SECTIONS = 8
Z = 16
BLOCK = 80
HALF = 40
TAPS = 9 * BLOCK
LANES = 128
CHUNKS = ((0, 1, 2, 3), (4, 5, 6, 7), (8, 9, 10, 11), (12, 13, 14, 15))
MESH = pl.DeviceIdType.MESH
F32 = jnp.float32
BF16 = jnp.bfloat16


def step_of(i):
    if i == 0:
        return Z // 2
    distance = Z // 2 - (i + 1) // 2
    return distance if i % 2 else Z - distance


def lane_ids(rows):
    return lax.broadcasted_iota(jnp.int32, (rows, LANES), 1)


def as_column(row):
    square = jnp.broadcast_to(row, (BLOCK, BLOCK))
    diagonal = lax.broadcasted_iota(jnp.int32, (BLOCK, BLOCK), 0) == lax.broadcasted_iota(
        jnp.int32, (BLOCK, BLOCK), 1
    )
    return jnp.sum(jnp.where(diagonal, square, 0.0), axis=1, keepdims=True)


def pack_column(column):
    left = jnp.broadcast_to(column[:HALF], (HALF, LANES))
    right = jnp.broadcast_to(column[HALF:], (HALF, LANES))
    return jnp.where(lane_ids(HALF) < CELLS, left, right)


def pack(block):
    return jnp.where(lane_ids(HALF) < CELLS, block[:HALF], pltpu.roll(block[HALF:], CELLS, 1))


def square_of(rows):
    short_lanes = LANES - rows.shape[1]
    if short_lanes:
        rows = jnp.concatenate([rows, jnp.zeros((rows.shape[0], short_lanes), F32)], axis=1)
    short = LANES - rows.shape[0]
    if short:
        rows = jnp.concatenate([rows, jnp.zeros((short, LANES), F32)], axis=0)
    return rows


def kernel(
    order_ref,
    time_ref,
    step_ref,
    latent_ref,
    stale_ref,
    weight_hbm,
    bias_ref,
    gain_ref,
    shift_ref,
    proj_ref,
    out_ref,
    weight_ref,
    turned_ref,
    gain_packed,
    shift_packed,
    extra_packed,
    halo_ref,
    x_ref,
    recv_ref,
    base_ref,
    send_ref,
    base_out_ref,
    back_ref,
    back_out_ref,
    weight_sem,
    recv_sem,
    base_sem,
    send_sem,
    base_out_sem,
    back_sem,
    back_out_sem,
):
    s = lax.axis_index("section")
    c = lax.axis_index("chan")
    r = lax.axis_index("rep")
    last = SECTIONS - 1
    is_last = s == last
    is_first = s == 0
    kind = jnp.where(is_last, 1, 0)
    target = jnp.where(is_last, last, s + 1)
    behind = jnp.maximum(s - 1, 0)

    weight_copy = pltpu.make_async_copy(weight_hbm, weight_ref, weight_sem)
    weight_copy.start()

    barrier = pltpu.get_barrier_semaphore()

    @pl.when(s > 0)
    def _():
        for i in range(Z):
            z = lax.rem(c + step_of(i) if i < Z - 1 else c, Z)
            pl.semaphore_signal(barrier, inc=1, device_id=(behind, z, r), device_id_type=MESH)

    @pl.when(is_last)
    def _():
        for i in range(Z - 1):
            z = lax.rem(c + step_of(i), Z)
            pl.semaphore_signal(barrier, inc=1, device_id=(s, z, r), device_id_type=MESH)

    @pl.when(s < last)
    def _():
        pl.semaphore_signal(barrier, inc=1, device_id=(s + 1, c, r), device_id_type=MESH)

    first_is_zero = order_ref[0] == 0

    gain_packed[...] = pack_column(as_column(gain_ref[...]))
    shift_packed[...] = pack_column(as_column(shift_ref[...]))

    for p in range(2):
        flat = square_of(latent_ref[p].astype(F32))
        x_ref[p] = pack(jnp.transpose(flat)[:BLOCK])

    below = jnp.zeros((W, BLOCK), F32)
    above = jnp.zeros((W, BLOCK), F32)
    for k in range(STALE):
        below = below + jnp.where(step_ref[0, 1] == k, stale_ref[k, 1, 0].astype(F32), 0.0)
        above = above + jnp.where(step_ref[0, 0] == k, stale_ref[k, 0, 1].astype(F32), 0.0)
    zero_rows = jnp.zeros((2 * W, BLOCK), F32)
    upper = jnp.where(first_is_zero, 0.0, above)
    lower = jnp.where(first_is_zero, below, 0.0)
    halo_ref[...] = jnp.transpose(square_of(jnp.concatenate([upper, zero_rows, lower], axis=0)))[
        :BLOCK
    ]

    weight_copy.wait()

    for j in range(C // LANES):
        turned_ref[pl.ds(LANES * j, LANES), :] = jnp.transpose(
            weight_ref[:, pl.ds(LANES * j, LANES)]
        )

    half = TDIM // 2
    lanes = lax.broadcasted_iota(jnp.int32, (8, TDIM), 1)
    index = jnp.where(lanes < half, lanes, lanes - half).astype(F32)
    angles = time_ref[0].astype(F32) * jnp.exp(index * (-math.log(10000.0) / half))
    emb = jnp.where(lanes < half, jnp.cos(angles), jnp.sin(angles))
    semb = (emb / (1.0 + jnp.exp(-emb))).astype(BF16).astype(F32)
    temb = jnp.sum(proj_ref[...].astype(F32) * semb[:1], axis=1, keepdims=True)
    extra_packed[...] = pack_column(as_column(bias_ref[...]) + temb)

    pl.semaphore_wait(barrier, jnp.where(is_first | is_last, Z, Z + 1))

    wide = lane_ids(BLOCK)
    column = lax.rem(wide, W)
    middle = (wide >= W) & (wide < 3 * W)
    half_lanes = lane_ids(HALF) < CELLS

    def remote(src, dst, send, recv, device):
        return pltpu.make_async_remote_copy(
            src_ref=src,
            dst_ref=dst,
            send_sem=send,
            recv_sem=recv,
            device_id=device,
            device_id_type=MESH,
        )

    def block_copy(q, i):
        return remote(
            send_ref.at[q, i],
            recv_ref.at[kind, q, i],
            send_sem.at[q, i],
            recv_sem.at[kind, q, i],
            (target, lax.rem(c + step_of(i), Z), r),
        )

    def base_copy(q):
        return remote(
            base_out_ref.at[q],
            base_ref.at[q],
            base_out_sem.at[q],
            base_sem.at[q],
            (jnp.minimum(s + 1, last), c, r),
        )

    def back_copy(q):
        return remote(
            back_out_ref.at[q],
            back_ref.at[q],
            back_out_sem.at[q],
            back_sem.at[q],
            (behind, c, r),
        )

    def gathered(which, q, start):
        total = start
        for i in range(Z - 2, -1, -1):
            slot = recv_ref.at[which, q, i]
            pltpu.make_async_copy(slot, slot, recv_sem.at[which, q, i]).wait()
            total = total + recv_ref[which, q, i].astype(F32)
        return total.astype(BF16)

    def group_mean(rows):
        summed = jnp.sum(rows, axis=0, keepdims=True)
        mask = half_lanes[:1]
        left = jnp.sum(jnp.where(mask, summed, 0.0), axis=1, keepdims=True)
        right = jnp.sum(jnp.where(mask, 0.0, summed), axis=1, keepdims=True)
        return jnp.where(mask, left, right) * (1.0 / (HALF * CELLS))

    for q in range(2):
        if q == 0:
            picked = jnp.where(first_is_zero, x_ref[0], x_ref[1])
            other = jnp.where(first_is_zero, x_ref[1], x_ref[0])
            x_ref[0] = picked
            x_ref[1] = other

        @pl.when(s > 0)
        def _():
            base = base_ref.at[q]
            pltpu.make_async_copy(base, base, base_sem.at[q]).wait()
            x_ref[q] = gathered(0, q, base_ref[q]).astype(F32)

        x = x_ref[q]
        mean = group_mean(x)
        centred = x - mean
        variance = group_mean(centred * centred)
        scaled = centred / jnp.sqrt(variance + 1e-05) * gain_packed[...] + shift_packed[...]
        hidden = (scaled / (1.0 + jnp.exp(-scaled))).astype(BF16).astype(F32)
        spread = jnp.concatenate([pltpu.roll(hidden, W, 1), pltpu.roll(hidden, 3 * W, 1)], axis=0)
        halo = halo_ref[...]
        extended = jnp.where(middle, spread, halo)
        if q == 0:
            turned_row = pltpu.roll(extended, CELLS, 1)
            halo_ref[...] = jnp.where(
                first_is_zero,
                jnp.where(wide < W, turned_row, 0.0),
                jnp.where(wide >= 3 * W, turned_row, 0.0),
            )
        shifted = [
            jnp.where(column == 0, 0.0, pltpu.roll(extended, 1, 1)),
            extended,
            jnp.where(column == W - 1, 0.0, pltpu.roll(extended, LANES - 1, 1)),
        ]
        taps = jnp.concatenate(
            [
                (shifted[b] if a == 0 else pltpu.roll(shifted[b], LANES - W * a, 1)).astype(BF16)
                for a in range(3)
                for b in range(3)
            ],
            axis=0,
        )
        for chunk in CHUNKS:
            rows = []
            for i in chunk:
                z = lax.rem(c + step_of(i), Z) if i < Z - 1 else c
                rows.append(turned_ref[pl.ds(pl.multiple_of(z * BLOCK, 16), BLOCK), :])
            product = jnp.dot(jnp.concatenate(rows, axis=0), taps, preferred_element_type=F32)
            for place, i in enumerate(chunk):
                part = pack(product[place * BLOCK : (place + 1) * BLOCK])
                if i < Z - 1:
                    send_ref[q, i] = part.astype(BF16)
                    block_copy(q, i).start()
                else:
                    base_out_ref[q] = x + part + extra_packed[...]

        @pl.when(s < last)
        def _():
            base_copy(q).start()

        @pl.when(s > 0)
        def _():
            back_out_ref[q] = x.astype(BF16)
            back_copy(q).start()

    results = []
    for q in range(2):

        @pl.when(s < last)
        def _():
            back = back_ref.at[q]
            pltpu.make_async_copy(back, back, back_sem.at[q]).wait()
            x_ref[q] = back_ref[q].astype(F32)

        @pl.when(is_last)
        def _():
            x_ref[q] = gathered(1, q, base_out_ref[q]).astype(F32)

        packed = x_ref[q]
        rows = square_of(jnp.concatenate([packed, pltpu.roll(packed, CELLS, 1)], axis=0))
        results.append(jnp.transpose(rows)[:CELLS, :BLOCK].astype(BF16))
    out_ref[0] = jnp.where(first_is_zero, results[0].astype(F32), results[1].astype(F32)).astype(
        BF16
    )
    out_ref[1] = jnp.where(first_is_zero, results[1].astype(F32), results[0].astype(F32)).astype(
        BF16
    )

    for q in range(2):
        for i in range(Z - 1):
            block_copy(q, i).wait_send()

        @pl.when(s < last)
        def _():
            base_copy(q).wait_send()

        @pl.when(s > 0)
        def _():
            back_copy(q).wait_send()


def on_device(
    latent,
    stale_rows,
    conv_weight,
    conv_bias,
    norm_gain,
    norm_shift,
    time_proj,
    patch_order,
    timestep,
    stale_step,
):
    vmem = pl.BlockSpec(memory_space=pltpu.VMEM)
    smem = pl.BlockSpec(memory_space=pltpu.SMEM)
    packed = pltpu.VMEM((HALF, LANES), F32)
    out = pl.pallas_call(
        kernel,
        out_shape=jax.ShapeDtypeStruct((2, CELLS, BLOCK), BF16),
        in_specs=[smem, smem, smem, vmem, vmem, pl.BlockSpec(memory_space=pl.ANY)] + [vmem] * 4,
        out_specs=vmem,
        scratch_shapes=[
            pltpu.VMEM((TAPS, C), BF16),
            pltpu.VMEM((C, TAPS), BF16),
            packed,
            packed,
            packed,
            pltpu.VMEM((BLOCK, LANES), F32),
            pltpu.VMEM((2, HALF, LANES), F32),
            pltpu.VMEM((2, 2, Z - 1, HALF, LANES), BF16),
            pltpu.VMEM((2, HALF, LANES), F32),
            pltpu.VMEM((2, Z - 1, HALF, LANES), BF16),
            pltpu.VMEM((2, HALF, LANES), F32),
            pltpu.VMEM((2, HALF, LANES), BF16),
            pltpu.VMEM((2, HALF, LANES), BF16),
            pltpu.SemaphoreType.DMA,
            pltpu.SemaphoreType.DMA((2, 2, Z - 1)),
            pltpu.SemaphoreType.DMA((2,)),
            pltpu.SemaphoreType.DMA((2, Z - 1)),
            pltpu.SemaphoreType.DMA((2,)),
            pltpu.SemaphoreType.DMA((2,)),
            pltpu.SemaphoreType.DMA((2,)),
        ],
        compiler_params=pltpu.CompilerParams(
            collective_id=0, has_side_effects=True, vmem_limit_bytes=32 * 1024 * 1024
        ),
        name="segments",
    )(
        patch_order,
        timestep,
        stale_step,
        jnp.transpose(latent, (0, 2, 1)),
        jnp.transpose(stale_rows[:, 0], (0, 1, 3, 4, 2)),
        conv_weight.reshape(TAPS, C),
        conv_bias,
        norm_gain,
        norm_shift,
        jnp.transpose(time_proj[0]),
    )
    return jnp.transpose(out, (0, 2, 1))[None]


def solution(mesh):
    placed = (
        P("rep", "chan", None),
        P(None, "section", "rep", "chan", None, None),
        P("section", None, "chan", None),
        P("section", "chan"),
        P("section", "chan"),
        P("section", "chan"),
        P("section", None, "chan"),
        P(),
        P("rep"),
        P("section", None),
    )
    return jax.shard_map(
        on_device,
        mesh=mesh,
        in_specs=placed,
        out_specs=P("section", "rep", "chan", None),
        check_vma=False,
    )
```

```python
import functools
import math

import jax
import jax.numpy as jnp
from jax import lax
from jax.experimental import pallas as pl
from jax.experimental.pallas import tpu as pltpu
from jax.sharding import PartitionSpec as P

C = 1280
TDIM = 320
W = 32
CELLS = 64
STALE = 4
SECTIONS = 8
Z = 16
BLOCK = 80
HALF = 40
PIECE = 256
TAPS = 9 * BLOCK
LANES = 128
OWN = Z - 1
FAR_CHUNKS = ((0,), (1, 2), (3, 4, 5, 6))
MIDDLE_CHUNKS = ((7, 8), (9, 10))
NEAR_CHUNK = (11, 12, 13, 14)
FAR = 7
MESH = pl.DeviceIdType.MESH
F32 = jnp.float32
BF16 = jnp.bfloat16


def step_of(i):
    if i == 0:
        return Z // 2
    distance = Z // 2 - (i + 1) // 2
    return distance if i % 2 else Z - distance


def lane_ids(rows):
    return lax.broadcasted_iota(jnp.int32, (rows, LANES), 1)


def as_column(row):
    square = jnp.broadcast_to(row, (BLOCK, BLOCK))
    diagonal = lax.broadcasted_iota(jnp.int32, (BLOCK, BLOCK), 0) == lax.broadcasted_iota(
        jnp.int32, (BLOCK, BLOCK), 1
    )
    return jnp.sum(jnp.where(diagonal, square, 0.0), axis=1, keepdims=True)


def pack_column(column):
    left = jnp.broadcast_to(column[:HALF], (HALF, LANES))
    right = jnp.broadcast_to(column[HALF:], (HALF, LANES))
    return jnp.where(lane_ids(HALF) < CELLS, left, right)


def pack(block):
    return jnp.where(lane_ids(HALF) < CELLS, block[:HALF], pltpu.roll(block[HALF:], CELLS, 1))


def square_of(rows):
    short_lanes = LANES - rows.shape[1]
    if short_lanes:
        rows = jnp.concatenate([rows, jnp.zeros((rows.shape[0], short_lanes), F32)], axis=1)
    short = LANES - rows.shape[0]
    if short:
        rows = jnp.concatenate([rows, jnp.zeros((short, LANES), F32)], axis=0)
    return rows


def kernel(
    order_hbm,
    time_hbm,
    step_hbm,
    latent_hbm,
    stale_hbm,
    weight_hbm,
    bias_hbm,
    gain_hbm,
    shift_hbm,
    proj_hbm,
    out_ref,
    order_ref,
    time_ref,
    step_ref,
    latent_ref,
    below_ref,
    above_ref,
    bias_ref,
    gain_ref,
    shift_ref,
    proj_ref,
    weight_ref,
    turned_ref,
    gain_packed,
    shift_packed,
    extra_packed,
    halo_ref,
    x_ref,
    recv_ref,
    base_ref,
    send_ref,
    base_out_ref,
    back_ref,
    back_out_ref,
    weight_sem,
    load_sem,
    recv_sem,
    base_sem,
    send_sem,
    base_out_sem,
    back_sem,
    back_out_sem,
):
    s = lax.axis_index("section")
    c = lax.axis_index("chan")
    r = lax.axis_index("rep")
    last = SECTIONS - 1
    is_last = s == last
    is_first = s == 0
    kind = jnp.where(is_last, 1, 0)
    target = jnp.where(is_last, last, s + 1)
    behind = jnp.maximum(s - 1, 0)

    loads = [
        pltpu.make_async_copy(src, dst, load_sem.at[i])
        for i, (src, dst) in enumerate(
            (
                (latent_hbm, latent_ref),
                (order_hbm, order_ref),
                (gain_hbm, gain_ref),
                (shift_hbm, shift_ref),
                (step_hbm, step_ref),
                (stale_hbm.at[:, 1, 0], below_ref),
                (stale_hbm.at[:, 0, 1], above_ref),
                (time_hbm, time_ref),
                (bias_hbm, bias_ref),
                (proj_hbm, proj_ref),
            )
        )
    ]
    weight_copies = [
        pltpu.make_async_copy(
            weight_hbm.at[:, pl.ds(PIECE * j, PIECE)],
            weight_ref.at[:, pl.ds(PIECE * j, PIECE)],
            weight_sem.at[j],
        )
        for j in range(C // PIECE)
    ]

    barrier = pltpu.get_barrier_semaphore()

    @pl.when(s > 0)
    def _():
        for i in range(Z):
            z = lax.rem(c + step_of(i) if i < Z - 1 else c, Z)
            pl.semaphore_signal(barrier, inc=1, device_id=(behind, z, r), device_id_type=MESH)

    @pl.when(is_last)
    def _():
        for i in range(Z - 1):
            z = lax.rem(c + step_of(i), Z)
            pl.semaphore_signal(barrier, inc=1, device_id=(s, z, r), device_id_type=MESH)

    @pl.when(s < last)
    def _():
        pl.semaphore_signal(barrier, inc=1, device_id=(s + 1, c, r), device_id_type=MESH)

    for load in loads[:7]:
        load.start()
    for copy in weight_copies:
        copy.start()
    for load in loads[7:]:
        load.start()

    for load in loads[:7]:
        load.wait()
    first_is_zero = order_ref[0] == 0

    gain_packed[...] = pack_column(as_column(gain_ref[...]))
    shift_packed[...] = pack_column(as_column(shift_ref[...]))

    @pl.when(is_first)
    def _():
        packed = [pack(jnp.transpose(square_of(latent_ref[p].astype(F32)))[:BLOCK]) for p in (0, 1)]
        x_ref[0] = jnp.where(first_is_zero, packed[0], packed[1])
        x_ref[1] = jnp.where(first_is_zero, packed[1], packed[0])

    below = jnp.zeros((W, BLOCK), F32)
    above = jnp.zeros((W, BLOCK), F32)
    for k in range(STALE):
        below = below + jnp.where(step_ref[0, 1] == k, below_ref[k].astype(F32), 0.0)
        above = above + jnp.where(step_ref[0, 0] == k, above_ref[k].astype(F32), 0.0)
    zero_rows = jnp.zeros((2 * W, BLOCK), F32)
    upper = jnp.where(first_is_zero, 0.0, above)
    lower = jnp.where(first_is_zero, below, 0.0)
    wide = lane_ids(BLOCK)
    column = lax.rem(wide, W)
    half_lanes = lane_ids(HALF) < CELLS

    def set_halo(halo):
        for b in range(3):
            moved = halo
            if b != 1:
                edge = 0 if b == 0 else W - 1
                moved = jnp.where(column == edge, 0.0, pltpu.roll(halo, (1 - b) % LANES, 1))
            for a in (0, 2):
                halo_ref[3 * a + b] = moved if a == 0 else pltpu.roll(moved, CELLS, 1)

    set_halo(
        jnp.transpose(square_of(jnp.concatenate([upper, zero_rows, lower], axis=0)))[:BLOCK]
    )

    for j in range(C // PIECE):
        weight_copies[j].wait()
        turned_ref[pl.ds(PIECE * j, PIECE), :] = jnp.transpose(
            weight_ref[:, pl.ds(PIECE * j, PIECE)]
        )
    for load in loads[7:]:
        load.wait()

    half = TDIM // 2
    lanes = lax.broadcasted_iota(jnp.int32, (8, TDIM), 1)
    index = jnp.where(lanes < half, lanes, lanes - half).astype(F32)
    angles = time_ref[0].astype(F32) * jnp.exp(index * (-math.log(10000.0) / half))
    emb = jnp.where(lanes < half, jnp.cos(angles), jnp.sin(angles))
    semb = (emb / (1.0 + jnp.exp(-emb))).astype(BF16).astype(F32)
    temb = jnp.sum(proj_ref[...].astype(F32) * semb[:1], axis=1, keepdims=True)
    extra_packed[...] = pack_column(as_column(bias_ref[...]) + temb)

    def remote(src, dst, send, recv, device):
        return pltpu.make_async_remote_copy(
            src_ref=src,
            dst_ref=dst,
            send_sem=send,
            recv_sem=recv,
            device_id=device,
            device_id_type=MESH,
        )

    def block_copy(q, i):
        return remote(
            send_ref.at[q, i],
            recv_ref.at[kind, q, i],
            send_sem.at[q, i],
            recv_sem.at[kind, q, i],
            (target, lax.rem(c + step_of(i), Z), r),
        )

    def base_copy(q):
        return remote(
            base_out_ref.at[q],
            base_ref.at[q],
            base_out_sem.at[q],
            base_sem.at[q],
            (jnp.minimum(s + 1, last), c, r),
        )

    def back_copy(q):
        return remote(
            back_out_ref.at[q],
            back_ref.at[q],
            back_out_sem.at[q],
            back_sem.at[q],
            (behind, c, r),
        )

    def gathered(which, q, start):
        total = start
        for i in range(Z - 2, -1, -1):
            slot = recv_ref.at[which, q, i]
            pltpu.make_async_copy(slot, slot, recv_sem.at[which, q, i]).wait()
            total = total + recv_ref[which, q, i].astype(F32)
        return total.astype(BF16)

    def group_mean(rows):
        summed = jnp.sum(rows, axis=0, keepdims=True)
        mask = half_lanes[:1]
        left = jnp.sum(jnp.where(mask, summed, 0.0), axis=1, keepdims=True)
        right = jnp.sum(jnp.where(mask, 0.0, summed), axis=1, keepdims=True)
        return jnp.where(mask, left, right) * (1.0 / (HALF * CELLS))

    def taps_of(q, x):
        mean = group_mean(x)
        centred = x - mean
        variance = group_mean(centred * centred)
        scaled = centred * (1.0 / jnp.sqrt(variance + 1e-05)) * gain_packed[...] + shift_packed[...]
        hidden = scaled / (1.0 + jnp.exp(-scaled))
        taps = []
        for a in range(3):
            for b in range(3):
                shift = W * (a - 1) + b - 1
                moved = jnp.concatenate(
                    [
                        pltpu.roll(hidden, -shift % LANES, 1) if shift else hidden,
                        pltpu.roll(hidden, (CELLS - shift) % LANES, 1),
                    ],
                    axis=0,
                )
                valid = None
                if a != 1:
                    valid = wide >= W if a == 0 else wide < W
                if b != 1:
                    inside = column != (0 if b == 0 else W - 1)
                    valid = inside if valid is None else valid & inside
                if valid is not None:
                    moved = jnp.where(valid, moved, 0.0 if a == 1 else halo_ref[3 * a + b])
                taps.append(moved.astype(BF16))
        return hidden, jnp.concatenate(taps, axis=0)

    def next_halo(hidden):
        spread = jnp.concatenate([pltpu.roll(hidden, W, 1), pltpu.roll(hidden, 3 * W, 1)], axis=0)
        turned_row = pltpu.roll(spread, CELLS, 1)
        set_halo(
            jnp.where(
                first_is_zero,
                jnp.where(wide < W, turned_row, 0.0),
                jnp.where(wide >= 3 * W, turned_row, 0.0),
            )
        )

    def multiply(q, taps, chunk):
        rows = []
        for i in chunk:
            z = c if i == OWN else lax.rem(c + step_of(i), Z)
            rows.append(turned_ref[pl.ds(pl.multiple_of(z * BLOCK, 16), BLOCK), :])
        product = jnp.dot(jnp.concatenate(rows, axis=0), taps, preferred_element_type=F32)
        parts = [pack(product[k * BLOCK : (k + 1) * BLOCK]) for k in range(len(chunk))]
        for i, part in zip(chunk, parts):
            if i != OWN:
                send_ref[q, i] = part.astype(BF16)
        return parts

    def start(q, chunk):
        for i in chunk:
            block_copy(q, i).start()

    def finish(q):
        for i in range(FAR):
            block_copy(q, i).wait_send()
        start(q, NEAR_CHUNK)

    @pl.when(is_first)
    def _():
        for q in range(2):
            x = x_ref[q]
            hidden, taps = taps_of(q, x)
            for chunk in FAR_CHUNKS + MIDDLE_CHUNKS + (NEAR_CHUNK,):
                multiply(q, taps, chunk)
            base_out_ref[q] = x + multiply(q, taps, (OWN,))[0] + extra_packed[...]
            if q == 0:
                next_halo(hidden)

    pl.semaphore_wait(barrier, jnp.where(is_first | is_last, Z, Z + 1))

    @pl.when(is_first)
    def _():
        for q in range(2):
            for chunk in FAR_CHUNKS + MIDDLE_CHUNKS:
                start(q, chunk)
            base_copy(q).start()
            finish(q)

    @pl.when(s > 0)
    def _():
        for q in range(2):
            base = base_ref.at[q]
            pltpu.make_async_copy(base, base, base_sem.at[q]).wait()
            x = gathered(0, q, base_ref[q]).astype(F32)
            hidden, taps = taps_of(q, x)
            for chunk in FAR_CHUNKS:
                multiply(q, taps, chunk)
                start(q, chunk)
            multiply(q, taps, MIDDLE_CHUNKS[0])
            start(q, MIDDLE_CHUNKS[0])
            base_out_ref[q] = x + multiply(q, taps, (OWN,))[0] + extra_packed[...]

            @pl.when(s < last)
            def _():
                base_copy(q).start()

            multiply(q, taps, MIDDLE_CHUNKS[1])
            start(q, MIDDLE_CHUNKS[1])
            back_out_ref[q] = x.astype(BF16)
            back_copy(q).start()
            multiply(q, taps, NEAR_CHUNK)
            if q == 0:
                next_halo(hidden)
            finish(q)

    results = []
    for q in range(2):

        @pl.when(s < last)
        def _():
            back = back_ref.at[q]
            pltpu.make_async_copy(back, back, back_sem.at[q]).wait()
            x_ref[q] = back_ref[q].astype(F32)

        @pl.when(is_last)
        def _():
            x_ref[q] = gathered(1, q, base_out_ref[q]).astype(F32)

        packed = x_ref[q]
        rows = square_of(jnp.concatenate([packed, pltpu.roll(packed, CELLS, 1)], axis=0))
        results.append(jnp.transpose(rows)[:CELLS, :BLOCK].astype(BF16))
    out_ref[0] = jnp.where(first_is_zero, results[0].astype(F32), results[1].astype(F32)).astype(
        BF16
    )
    out_ref[1] = jnp.where(first_is_zero, results[1].astype(F32), results[0].astype(F32)).astype(
        BF16
    )

    for q in range(2):
        for i in range(FAR, Z - 1):
            block_copy(q, i).wait_send()

        @pl.when(s < last)
        def _():
            base_copy(q).wait_send()

        @pl.when(s > 0)
        def _():
            back_copy(q).wait_send()


def on_device(
    latent,
    stale_rows,
    conv_weight,
    conv_bias,
    norm_gain,
    norm_shift,
    time_proj,
    patch_order,
    timestep,
    stale_step,
):
    packed = pltpu.VMEM((HALF, LANES), F32)
    out = pl.pallas_call(
        kernel,
        out_shape=pltpu.VMEM((2, CELLS, BLOCK), BF16),
        in_specs=[pl.BlockSpec(memory_space=pltpu.HBM)] * 10,
        out_specs=pl.BlockSpec(memory_space=pltpu.VMEM),
        scratch_shapes=[
            pltpu.SMEM((2,), jnp.int32),
            pltpu.SMEM((1,), jnp.int32),
            pltpu.SMEM((1, 2), jnp.int32),
            pltpu.VMEM((2, CELLS, BLOCK), BF16),
            pltpu.VMEM((STALE, W, BLOCK), BF16),
            pltpu.VMEM((STALE, W, BLOCK), BF16),
            pltpu.VMEM((1, BLOCK), F32),
            pltpu.VMEM((1, BLOCK), F32),
            pltpu.VMEM((1, BLOCK), F32),
            pltpu.VMEM((BLOCK, TDIM), BF16),
            pltpu.VMEM((TAPS, C), BF16),
            pltpu.VMEM((C, TAPS), BF16),
            packed,
            packed,
            packed,
            pltpu.VMEM((9, BLOCK, LANES), F32),
            pltpu.VMEM((2, HALF, LANES), F32),
            pltpu.VMEM((2, 2, Z - 1, HALF, LANES), BF16),
            pltpu.VMEM((2, HALF, LANES), F32),
            pltpu.VMEM((2, Z - 1, HALF, LANES), BF16),
            pltpu.VMEM((2, HALF, LANES), F32),
            pltpu.VMEM((2, HALF, LANES), BF16),
            pltpu.VMEM((2, HALF, LANES), BF16),
            pltpu.SemaphoreType.DMA((C // PIECE,)),
            pltpu.SemaphoreType.DMA((10,)),
            pltpu.SemaphoreType.DMA((2, 2, Z - 1)),
            pltpu.SemaphoreType.DMA((2,)),
            pltpu.SemaphoreType.DMA((2, Z - 1)),
            pltpu.SemaphoreType.DMA((2,)),
            pltpu.SemaphoreType.DMA((2,)),
            pltpu.SemaphoreType.DMA((2,)),
        ],
        compiler_params=pltpu.CompilerParams(
            collective_id=0, has_side_effects=True, vmem_limit_bytes=60 * 1024 * 1024
        ),
        name="segments",
    )(
        patch_order,
        timestep,
        stale_step,
        jnp.transpose(latent, (0, 2, 1)),
        jnp.transpose(stale_rows[:, 0], (0, 1, 3, 4, 2)),
        conv_weight.reshape(TAPS, C),
        conv_bias,
        norm_gain,
        norm_shift,
        jnp.transpose(time_proj[0]),
    )
    return jnp.transpose(out, (0, 2, 1))[None]


def solution(mesh):
    placed = (
        P("rep", "chan", None),
        P(None, "section", "rep", "chan", None, None),
        P("section", None, "chan", None),
        P("section", "chan"),
        P("section", "chan"),
        P("section", "chan"),
        P("section", None, "chan"),
        P(),
        P("rep"),
        P("section", None),
    )
    return jax.shard_map(
        on_device,
        mesh=mesh,
        in_specs=placed,
        out_specs=P("section", "rep", "chan", None),
        check_vma=False,
    )
```

```python
import functools
import math

import jax
import jax.numpy as jnp
from jax import lax
from jax.experimental import pallas as pl
from jax.experimental.pallas import tpu as pltpu
from jax.sharding import PartitionSpec as P

C = 1280
TDIM = 320
W = 32
CELLS = 64
STALE = 4
SECTIONS = 8
Z = 16
BLOCK = 80
HALF = 40
PIECE = 256
TAPS = 9 * BLOCK
LANES = 128
OWN = Z - 1
FAR_CHUNKS = ((0,), (1, 2), (3, 4, 5, 6))
MIDDLE_CHUNKS = ((7, 8), (9, 10))
NEAR_CHUNK = (11, 12, 13, 14)
FAR = 7
PAUSE = 6
MESH = pl.DeviceIdType.MESH
F32 = jnp.float32
BF16 = jnp.bfloat16


def step_of(i):
    if i == 0:
        return Z // 2
    distance = Z // 2 - (i + 1) // 2
    return distance if i % 2 else Z - distance


def odd(z):
    return lax.rem(z, 2) == 1


def holder(t, z):
    moved = jnp.where(t < 6, t + 2, t - 2)
    return jnp.where(odd(z) & (t >= 4), moved, t)


def section_of(s, z):
    taken = jnp.where(s < 6, s + 2, s - 2)
    return jnp.where(odd(z) & (s >= 4), taken, s)


def lane_ids(rows):
    return lax.broadcasted_iota(jnp.int32, (rows, LANES), 1)


def as_column(row):
    square = jnp.broadcast_to(row, (BLOCK, BLOCK))
    diagonal = lax.broadcasted_iota(jnp.int32, (BLOCK, BLOCK), 0) == lax.broadcasted_iota(
        jnp.int32, (BLOCK, BLOCK), 1
    )
    return jnp.sum(jnp.where(diagonal, square, 0.0), axis=1, keepdims=True)


def pack_column(column):
    left = jnp.broadcast_to(column[:HALF], (HALF, LANES))
    right = jnp.broadcast_to(column[HALF:], (HALF, LANES))
    return jnp.where(lane_ids(HALF) < CELLS, left, right)


def pack(block):
    return jnp.where(lane_ids(HALF) < CELLS, block[:HALF], pltpu.roll(block[HALF:], CELLS, 1))


def square_of(rows):
    short_lanes = LANES - rows.shape[1]
    if short_lanes:
        rows = jnp.concatenate([rows, jnp.zeros((rows.shape[0], short_lanes), F32)], axis=1)
    short = LANES - rows.shape[0]
    if short:
        rows = jnp.concatenate([rows, jnp.zeros((short, LANES), F32)], axis=0)
    return rows


def kernel(
    order_hbm,
    time_hbm,
    step_hbm,
    latent_hbm,
    stale_hbm,
    weight_hbm,
    bias_hbm,
    gain_hbm,
    shift_hbm,
    proj_hbm,
    out_ref,
    order_ref,
    time_ref,
    step_ref,
    latent_ref,
    below_ref,
    above_ref,
    bias_ref,
    gain_ref,
    shift_ref,
    proj_ref,
    weight_ref,
    turned_ref,
    own_packed,
    packed_ref,
    own_halo,
    given_halo,
    halo_ref,
    x_ref,
    recv_ref,
    base_ref,
    send_ref,
    base_out_ref,
    back_ref,
    back_out_ref,
    weight_sem,
    load_sem,
    move_out_sem,
    move_sem,
    pass_out_sem,
    pass_sem,
    turn_sem,
    recv_sem,
    base_sem,
    send_sem,
    base_out_sem,
    back_sem,
    back_out_sem,
):
    s = lax.axis_index("section")
    c = lax.axis_index("chan")
    r = lax.axis_index("rep")
    last = SECTIONS - 1
    is_first = s == 0
    role = section_of(s, c)
    host = holder(s, c)
    swapped = role != s
    core = lax.rem(s, 2)
    ends = role == last
    stays = ends & (s == last)
    kind = jnp.where(ends, 1, 0)
    ahead = jnp.minimum(role + 1, last)
    behind = jnp.maximum(role - 1, 0)

    def target(z):
        return jnp.where(ends, last, holder(ahead, z))

    loads = [
        pltpu.make_async_copy(src, dst, load_sem.at[i])
        for i, (src, dst) in enumerate(
            (
                (latent_hbm, latent_ref),
                (order_hbm, order_ref),
                (gain_hbm, gain_ref),
                (shift_hbm, shift_ref),
                (step_hbm, step_ref),
                (stale_hbm.at[:, 1, 0], below_ref),
                (stale_hbm.at[:, 0, 1], above_ref),
                (time_hbm, time_ref),
                (bias_hbm, bias_ref),
                (proj_hbm, proj_ref),
            )
        )
    ]
    weight_copy = pltpu.make_async_copy(weight_hbm, weight_ref, weight_sem)

    def greet(section, z):
        pl.semaphore_signal(barrier, inc=1, device_id=(section, z, r), device_id_type=MESH)

    barrier = pltpu.get_barrier_semaphore()

    @pl.when(role > 0)
    def _():
        for i in range(Z):
            z = lax.rem(c + step_of(i), Z) if i < OWN else c
            greet(holder(behind, z), z)

    @pl.when(s == last)
    def _():
        for i in range(Z - 1):
            z = lax.rem(c + step_of(i), Z)
            greet(holder(last, z), z)

    @pl.when((s == last) & swapped)
    def _():
        greet(holder(last, c), c)

    @pl.when(s < last)
    def _():
        greet(holder(s + 1, c), c)

    @pl.when(swapped)
    def _():
        greet(role, c)
        for i in range(1, 4):
            pl.semaphore_signal(
                barrier, inc=1, device_id=(s, c, lax.rem(r + i, 4)), device_id_type=MESH
            )

    @pl.when(swapped & (core == 1))
    def _():
        greet(s - 1, c)

    for load in loads[:7]:
        load.start()

    @pl.when(jnp.logical_not(swapped))
    def _():
        weight_copy.start()

    for load in loads[7:]:
        load.start()

    for load in loads[:7]:
        load.wait()
    first_is_zero = order_ref[0] == 0

    own_packed[0] = pack_column(as_column(gain_ref[...]))
    own_packed[1] = pack_column(as_column(shift_ref[...]))

    @pl.when(is_first)
    def _():
        packed = [pack(jnp.transpose(square_of(latent_ref[p].astype(F32)))[:BLOCK]) for p in (0, 1)]
        x_ref[0] = jnp.where(first_is_zero, packed[0], packed[1])
        x_ref[1] = jnp.where(first_is_zero, packed[1], packed[0])

    below = jnp.zeros((W, BLOCK), F32)
    above = jnp.zeros((W, BLOCK), F32)
    for k in range(STALE):
        below = below + jnp.where(step_ref[0, 1] == k, below_ref[k].astype(F32), 0.0)
        above = above + jnp.where(step_ref[0, 0] == k, above_ref[k].astype(F32), 0.0)
    zero_rows = jnp.zeros((2 * W, BLOCK), F32)
    upper = jnp.where(first_is_zero, 0.0, above)
    lower = jnp.where(first_is_zero, below, 0.0)
    wide = lane_ids(BLOCK)
    column = lax.rem(wide, W)
    half_lanes = lane_ids(HALF) < CELLS

    def set_halo(halo):
        for b in range(3):
            moved = halo
            if b != 1:
                edge = 0 if b == 0 else W - 1
                moved = jnp.where(column == edge, 0.0, pltpu.roll(halo, (1 - b) % LANES, 1))
            for a in (0, 2):
                halo_ref[3 * a + b] = moved if a == 0 else pltpu.roll(moved, CELLS, 1)

    own_halo[...] = jnp.transpose(
        square_of(jnp.concatenate([upper, zero_rows, lower], axis=0))
    )[:BLOCK]

    for load in loads[7:]:
        load.wait()

    half = TDIM // 2
    lanes = lax.broadcasted_iota(jnp.int32, (8, TDIM), 1)
    index = jnp.where(lanes < half, lanes, lanes - half).astype(F32)
    angles = time_ref[0].astype(F32) * jnp.exp(index * (-math.log(10000.0) / half))
    emb = jnp.where(lanes < half, jnp.cos(angles), jnp.sin(angles))
    semb = (emb / (1.0 + jnp.exp(-emb))).astype(BF16).astype(F32)
    temb = jnp.sum(proj_ref[...].astype(F32) * semb[:1], axis=1, keepdims=True)
    own_packed[2] = pack_column(as_column(bias_ref[...]) + temb)

    def turn():
        for j in range(C // PIECE):
            turned_ref[pl.ds(PIECE * j, PIECE), :] = jnp.transpose(
                weight_ref[:, :, pl.ds(PIECE * j, PIECE)].reshape(TAPS, PIECE)
            )

    @pl.when(jnp.logical_not(swapped))
    def _():
        packed_ref[...] = own_packed[...]
        set_halo(own_halo[...])
        weight_copy.wait()
        turn()

    def remote(src, dst, send, recv, device):
        return pltpu.make_async_remote_copy(
            src_ref=src,
            dst_ref=dst,
            send_sem=send,
            recv_sem=recv,
            device_id=device,
            device_id_type=MESH,
        )

    def block_copy(q, i):
        return remote(
            send_ref.at[q, i],
            recv_ref.at[kind, q, i],
            send_sem.at[q, i],
            recv_sem.at[kind, q, i],
            (target(lax.rem(c + step_of(i), Z)), lax.rem(c + step_of(i), Z), r),
        )

    def base_copy(q):
        return remote(
            base_out_ref.at[q],
            base_ref.at[kind, q],
            base_out_sem.at[q],
            base_sem.at[kind, q],
            (target(c), c, r),
        )

    def back_copy(q):
        return remote(
            back_out_ref.at[q],
            back_ref.at[q],
            back_out_sem.at[q],
            back_sem.at[q],
            (behind, c, r),
        )

    def gathered(which, q, total, between=None):
        for i in range(Z - 2, -1, -1):
            if between is not None and i == PAUSE:
                between()
            slot = recv_ref.at[which, q, i]
            pltpu.make_async_copy(slot, slot, recv_sem.at[which, q, i]).wait()
            total = total + recv_ref[which, q, i].astype(F32)
        return total.astype(BF16)

    def group_mean(rows):
        summed = jnp.sum(rows, axis=0, keepdims=True)
        mask = half_lanes[:1]
        left = jnp.sum(jnp.where(mask, summed, 0.0), axis=1, keepdims=True)
        right = jnp.sum(jnp.where(mask, 0.0, summed), axis=1, keepdims=True)
        return jnp.where(mask, left, right) * (1.0 / (HALF * CELLS))

    def taps_of(q, x):
        mean = group_mean(x)
        centred = x - mean
        variance = group_mean(centred * centred)
        scaled = centred * (1.0 / jnp.sqrt(variance + 1e-05)) * packed_ref[0] + packed_ref[1]
        hidden = scaled / (1.0 + jnp.exp(-scaled))
        taps = []
        for a in range(3):
            for b in range(3):
                shift = W * (a - 1) + b - 1
                moved = jnp.concatenate(
                    [
                        pltpu.roll(hidden, -shift % LANES, 1) if shift else hidden,
                        pltpu.roll(hidden, (CELLS - shift) % LANES, 1),
                    ],
                    axis=0,
                )
                valid = None
                if a != 1:
                    valid = wide >= W if a == 0 else wide < W
                if b != 1:
                    inside = column != (0 if b == 0 else W - 1)
                    valid = inside if valid is None else valid & inside
                if valid is not None:
                    moved = jnp.where(valid, moved, 0.0 if a == 1 else halo_ref[3 * a + b])
                taps.append(moved.astype(BF16))
        return hidden, jnp.concatenate(taps, axis=0)

    def next_halo(hidden):
        spread = jnp.concatenate([pltpu.roll(hidden, W, 1), pltpu.roll(hidden, 3 * W, 1)], axis=0)
        turned_row = pltpu.roll(spread, CELLS, 1)
        set_halo(
            jnp.where(
                first_is_zero,
                jnp.where(wide < W, turned_row, 0.0),
                jnp.where(wide >= 3 * W, turned_row, 0.0),
            )
        )

    def multiply(q, taps, chunk):
        rows = []
        for i in chunk:
            z = c if i == OWN else lax.rem(c + step_of(i), Z)
            rows.append(turned_ref[pl.ds(pl.multiple_of(z * BLOCK, 16), BLOCK), :])
        product = jnp.dot(jnp.concatenate(rows, axis=0), taps, preferred_element_type=F32)
        parts = [pack(product[k * BLOCK : (k + 1) * BLOCK]) for k in range(len(chunk))]
        for i, part in zip(chunk, parts):
            if i != OWN:
                send_ref[q, i] = part.astype(BF16)
        return parts

    def start(q, chunk):
        for i in chunk:
            block_copy(q, i).start()

    def finish(q):
        for i in range(FAR):
            block_copy(q, i).wait_send()
        start(q, NEAR_CHUNK)

    @pl.when(is_first)
    def _():
        for q in range(2):
            x = x_ref[q]
            hidden, taps = taps_of(q, x)
            for chunk in FAR_CHUNKS + MIDDLE_CHUNKS + (NEAR_CHUNK,):
                multiply(q, taps, chunk)
            base_out_ref[q] = x + multiply(q, taps, (OWN,))[0] + packed_ref[2]
            if q == 0:
                next_halo(hidden)

    greeted = jnp.where(stays, Z - 1, Z) + jnp.where(role > 0, 1, 0)
    greeted = greeted + jnp.where(swapped, jnp.where(core == 0, 5, 4), 0)
    pl.semaphore_wait(barrier, greeted)

    @pl.when(swapped)
    def _():
        moves = [
            remote(src, dst, move_out_sem.at[i], move_sem.at[i], (host, c, r))
            for i, (src, dst) in enumerate(
                (
                    (weight_hbm.at[2 * r], weight_ref.at[2 * r]),
                    (weight_hbm.at[2 * r + 1], weight_ref.at[2 * r + 1]),
                    (weight_hbm.at[8], weight_ref.at[8]),
                    (own_packed, packed_ref),
                    (own_halo, given_halo),
                )
            )
        ]

        @pl.when(core == 1)
        def _():
            pl.semaphore_wait(turn_sem, 1)

        for copy in moves:
            copy.start()

        def passed(i, j):
            return remote(
                weight_ref.at[2 * r + j],
                weight_ref.at[2 * r + j],
                pass_out_sem.at[i - 1, j],
                pass_sem.at[i - 1, j],
                (s, c, lax.rem(r + i, 4)),
            )

        for j in range(2):
            moves[j].wait_recv()
            for i in (2, 1, 3):
                passed(i, j).start()
        for copy in moves:
            copy.wait_send()

        @pl.when(core == 0)
        def _():
            pl.semaphore_signal(turn_sem, inc=1, device_id=(s + 1, c, r), device_id_type=MESH)

        for copy in moves[2:]:
            copy.wait_recv()
        set_halo(given_halo[...])
        for j in range(2):
            for i in range(1, 4):
                passed(i, j).wait_send()
                slot = weight_ref.at[2 * lax.rem(r + 4 - i, 4) + j]
                pltpu.make_async_copy(slot, slot, pass_sem.at[i - 1, j]).wait()
        turn()

    @pl.when(is_first)
    def _():
        for q in range(2):
            for chunk in FAR_CHUNKS + MIDDLE_CHUNKS:
                start(q, chunk)
            base_copy(q).start()
            finish(q)

    @pl.when(s > 0)
    def _():
        for q in range(2):
            base = base_ref.at[0, q]
            pltpu.make_async_copy(base, base, base_sem.at[0, q]).wait()
            near = functools.partial(start, 0, NEAR_CHUNK) if q else None
            x = gathered(0, q, base_ref[0, q], near).astype(F32)
            hidden, taps = taps_of(q, x)
            for chunk in FAR_CHUNKS:
                multiply(q, taps, chunk)
                start(q, chunk)
            multiply(q, taps, MIDDLE_CHUNKS[0])
            start(q, MIDDLE_CHUNKS[0])
            base_out_ref[q] = x + multiply(q, taps, (OWN,))[0] + packed_ref[2]

            @pl.when(jnp.logical_not(stays))
            def _():
                base_copy(q).start()

            multiply(q, taps, MIDDLE_CHUNKS[1])
            start(q, MIDDLE_CHUNKS[1])
            back_out_ref[q] = x.astype(BF16)
            back_copy(q).start()
            multiply(q, taps, NEAR_CHUNK)
            if q == 0:
                next_halo(hidden)
            else:
                finish(q)

    results = []
    for q in range(2):

        @pl.when(s < last)
        def _():
            back = back_ref.at[q]
            pltpu.make_async_copy(back, back, back_sem.at[q]).wait()
            x_ref[q] = back_ref[q].astype(F32)

        @pl.when(stays)
        def _():
            x_ref[q] = base_out_ref[q]

        @pl.when((s == last) & jnp.logical_not(stays))
        def _():
            base = base_ref.at[1, q]
            pltpu.make_async_copy(base, base, base_sem.at[1, q]).wait()
            x_ref[q] = base_ref[1, q]

        @pl.when(s == last)
        def _():
            x_ref[q] = gathered(1, q, x_ref[q]).astype(F32)

        packed = x_ref[q]
        rows = square_of(jnp.concatenate([packed, pltpu.roll(packed, CELLS, 1)], axis=0))
        results.append(jnp.transpose(rows)[:CELLS, :BLOCK].astype(BF16))
    out_ref[0] = jnp.where(first_is_zero, results[0].astype(F32), results[1].astype(F32)).astype(
        BF16
    )
    out_ref[1] = jnp.where(first_is_zero, results[1].astype(F32), results[0].astype(F32)).astype(
        BF16
    )

    for q in range(2):
        for i in range(FAR, Z - 1):
            block_copy(q, i).wait_send()
        if q == 0:

            @pl.when(s > 0)
            def _():
                for i in range(FAR):
                    block_copy(0, i).wait_send()

        @pl.when(jnp.logical_not(stays))
        def _():
            base_copy(q).wait_send()

        @pl.when(s > 0)
        def _():
            back_copy(q).wait_send()


def on_device(
    latent,
    stale_rows,
    conv_weight,
    conv_bias,
    norm_gain,
    norm_shift,
    time_proj,
    patch_order,
    timestep,
    stale_step,
):
    out = pl.pallas_call(
        kernel,
        out_shape=pltpu.VMEM((2, CELLS, BLOCK), BF16),
        in_specs=[pl.BlockSpec(memory_space=pltpu.HBM)] * 10,
        out_specs=pl.BlockSpec(memory_space=pltpu.VMEM),
        scratch_shapes=[
            pltpu.SMEM((2,), jnp.int32),
            pltpu.SMEM((1,), jnp.int32),
            pltpu.SMEM((1, 2), jnp.int32),
            pltpu.VMEM((2, CELLS, BLOCK), BF16),
            pltpu.VMEM((STALE, W, BLOCK), BF16),
            pltpu.VMEM((STALE, W, BLOCK), BF16),
            pltpu.VMEM((1, BLOCK), F32),
            pltpu.VMEM((1, BLOCK), F32),
            pltpu.VMEM((1, BLOCK), F32),
            pltpu.VMEM((BLOCK, TDIM), BF16),
            pltpu.VMEM((9, BLOCK, C), BF16),
            pltpu.VMEM((C, TAPS), BF16),
            pltpu.VMEM((3, HALF, LANES), F32),
            pltpu.VMEM((3, HALF, LANES), F32),
            pltpu.VMEM((BLOCK, LANES), F32),
            pltpu.VMEM((BLOCK, LANES), F32),
            pltpu.VMEM((9, BLOCK, LANES), F32),
            pltpu.VMEM((2, HALF, LANES), F32),
            pltpu.VMEM((2, 2, Z - 1, HALF, LANES), BF16),
            pltpu.VMEM((2, 2, HALF, LANES), F32),
            pltpu.VMEM((2, Z - 1, HALF, LANES), BF16),
            pltpu.VMEM((2, HALF, LANES), F32),
            pltpu.VMEM((2, HALF, LANES), BF16),
            pltpu.VMEM((2, HALF, LANES), BF16),
            pltpu.SemaphoreType.DMA,
            pltpu.SemaphoreType.DMA((10,)),
            pltpu.SemaphoreType.DMA((5,)),
            pltpu.SemaphoreType.DMA((5,)),
            pltpu.SemaphoreType.DMA((3, 2)),
            pltpu.SemaphoreType.DMA((3, 2)),
            pltpu.SemaphoreType.REGULAR,
            pltpu.SemaphoreType.DMA((2, 2, Z - 1)),
            pltpu.SemaphoreType.DMA((2, 2)),
            pltpu.SemaphoreType.DMA((2, Z - 1)),
            pltpu.SemaphoreType.DMA((2,)),
            pltpu.SemaphoreType.DMA((2,)),
            pltpu.SemaphoreType.DMA((2,)),
        ],
        compiler_params=pltpu.CompilerParams(
            collective_id=0, has_side_effects=True, vmem_limit_bytes=60 * 1024 * 1024
        ),
        name="segments",
    )(
        patch_order,
        timestep,
        stale_step,
        jnp.transpose(latent, (0, 2, 1)),
        jnp.transpose(stale_rows[:, 0], (0, 1, 3, 4, 2)),
        conv_weight[0],
        conv_bias,
        norm_gain,
        norm_shift,
        jnp.transpose(time_proj[0]),
    )
    return jnp.transpose(out, (0, 2, 1))[None]


def solution(mesh):
    placed = (
        P("rep", "chan", None),
        P(None, "section", "rep", "chan", None, None),
        P("section", None, "chan", None),
        P("section", "chan"),
        P("section", "chan"),
        P("section", "chan"),
        P("section", None, "chan"),
        P(),
        P("rep"),
        P("section", None),
    )
    return jax.shard_map(
        on_device,
        mesh=mesh,
        in_specs=placed,
        out_specs=P("section", "rep", "chan", None),
        check_vma=False,
    )
```

```python
import functools
import math

import jax
import jax.numpy as jnp
from jax import lax
from jax.experimental import pallas as pl
from jax.experimental.pallas import tpu as pltpu
from jax.sharding import PartitionSpec as P

C = 1280
TDIM = 320
W = 32
CELLS = 64
STALE = 4
SECTIONS = 8
Z = 16
BLOCK = 80
HALF = 40
PIECE = 256
TAPS = 9 * BLOCK
LANES = 128
OWN = Z - 1
FAR_CHUNKS = ((0,), (1, 2), (3, 4, 5, 6))
MIDDLE_CHUNKS = ((7, 8), (9, 10))
NEAR_CHUNK = (11, 12, 13, 14)
FAR = 7
PAUSE = 6
MESH = pl.DeviceIdType.MESH
F32 = jnp.float32
BF16 = jnp.bfloat16


def step_of(i):
    if i == 0:
        return Z // 2
    distance = Z // 2 - (i + 1) // 2
    return distance if i % 2 else Z - distance


def odd(z):
    return lax.rem(z, 2) == 1


def holder(t, z):
    moved = jnp.where(t < 6, t + 2, t - 2)
    return jnp.where(odd(z) & (t >= 4), moved, t)


def section_of(s, z):
    taken = jnp.where(s < 6, s + 2, s - 2)
    return jnp.where(odd(z) & (s >= 4), taken, s)


def lane_ids(rows):
    return lax.broadcasted_iota(jnp.int32, (rows, LANES), 1)


def as_column(row):
    square = jnp.broadcast_to(row, (BLOCK, BLOCK))
    diagonal = lax.broadcasted_iota(jnp.int32, (BLOCK, BLOCK), 0) == lax.broadcasted_iota(
        jnp.int32, (BLOCK, BLOCK), 1
    )
    return jnp.sum(jnp.where(diagonal, square, 0.0), axis=1, keepdims=True)


def pack_column(column):
    left = jnp.broadcast_to(column[:HALF], (HALF, LANES))
    right = jnp.broadcast_to(column[HALF:], (HALF, LANES))
    return jnp.where(lane_ids(HALF) < CELLS, left, right)


def pack(block):
    return jnp.where(lane_ids(HALF) < CELLS, block[:HALF], pltpu.roll(block[HALF:], CELLS, 1))


def square_of(rows):
    short_lanes = LANES - rows.shape[1]
    if short_lanes:
        rows = jnp.concatenate([rows, jnp.zeros((rows.shape[0], short_lanes), F32)], axis=1)
    short = LANES - rows.shape[0]
    if short:
        rows = jnp.concatenate([rows, jnp.zeros((short, LANES), F32)], axis=0)
    return rows


def kernel(
    order_hbm,
    time_hbm,
    step_hbm,
    latent_hbm,
    stale_hbm,
    weight_hbm,
    bias_hbm,
    gain_hbm,
    shift_hbm,
    proj_hbm,
    out_ref,
    order_ref,
    time_ref,
    step_ref,
    latent_ref,
    below_ref,
    above_ref,
    bias_ref,
    gain_ref,
    shift_ref,
    proj_ref,
    weight_ref,
    turned_ref,
    own_packed,
    packed_ref,
    own_halo,
    given_halo,
    halo_ref,
    x_ref,
    recv_ref,
    base_ref,
    send_ref,
    base_out_ref,
    back_ref,
    back_out_ref,
    weight_sem,
    load_sem,
    move_out_sem,
    move_sem,
    pass_out_sem,
    pass_sem,
    turn_sem,
    recv_sem,
    base_sem,
    send_sem,
    base_out_sem,
    back_sem,
    back_out_sem,
):
    s = lax.axis_index("section")
    c = lax.axis_index("chan")
    r = lax.axis_index("rep")
    last = SECTIONS - 1
    is_first = s == 0
    role = section_of(s, c)
    host = holder(s, c)
    swapped = role != s
    core = lax.rem(s, 2)
    ends = role == last
    stays = ends & (s == last)
    kind = jnp.where(ends, 1, 0)
    ahead = jnp.minimum(role + 1, last)
    behind = jnp.maximum(role - 1, 0)

    def target(z):
        return jnp.where(ends, last, holder(ahead, z))

    loads = [
        pltpu.make_async_copy(src, dst, load_sem.at[i])
        for i, (src, dst) in enumerate(
            (
                (latent_hbm, latent_ref),
                (order_hbm, order_ref),
                (gain_hbm, gain_ref),
                (shift_hbm, shift_ref),
                (step_hbm, step_ref),
                (stale_hbm.at[:, 1, 0], below_ref),
                (stale_hbm.at[:, 0, 1], above_ref),
                (time_hbm, time_ref),
                (bias_hbm, bias_ref),
                (proj_hbm, proj_ref),
            )
        )
    ]
    weight_copy = pltpu.make_async_copy(weight_hbm, weight_ref, weight_sem)

    def greet(section, z):
        pl.semaphore_signal(barrier, inc=1, device_id=(section, z, r), device_id_type=MESH)

    barrier = pltpu.get_barrier_semaphore()

    @pl.when(role > 0)
    def _():
        for i in range(Z):
            z = lax.rem(c + step_of(i), Z) if i < OWN else c
            greet(holder(behind, z), z)

    @pl.when(s == last)
    def _():
        for i in range(Z - 1):
            z = lax.rem(c + step_of(i), Z)
            greet(holder(last, z), z)

    @pl.when((s == last) & swapped)
    def _():
        greet(holder(last, c), c)

    @pl.when(s < last)
    def _():
        greet(holder(s + 1, c), c)

    @pl.when(swapped)
    def _():
        greet(role, c)
        for i in range(1, 4):
            pl.semaphore_signal(
                barrier, inc=1, device_id=(s, c, lax.rem(r + i, 4)), device_id_type=MESH
            )

    @pl.when(swapped & (core == 1))
    def _():
        greet(s - 1, c)

    for load in loads[:7]:
        load.start()

    @pl.when(jnp.logical_not(swapped))
    def _():
        weight_copy.start()

    for load in loads[7:]:
        load.start()

    for load in loads[:7]:
        load.wait()
    first_is_zero = order_ref[0] == 0

    own_packed[0] = pack_column(as_column(gain_ref[...]))
    own_packed[1] = pack_column(as_column(shift_ref[...]))

    @pl.when(is_first)
    def _():
        packed = [pack(jnp.transpose(square_of(latent_ref[p].astype(F32)))[:BLOCK]) for p in (0, 1)]
        x_ref[0] = jnp.where(first_is_zero, packed[0], packed[1])
        x_ref[1] = jnp.where(first_is_zero, packed[1], packed[0])

    below = jnp.zeros((W, BLOCK), F32)
    above = jnp.zeros((W, BLOCK), F32)
    for k in range(STALE):
        below = below + jnp.where(step_ref[0, 1] == k, below_ref[k].astype(F32), 0.0)
        above = above + jnp.where(step_ref[0, 0] == k, above_ref[k].astype(F32), 0.0)
    zero_rows = jnp.zeros((2 * W, BLOCK), F32)
    upper = jnp.where(first_is_zero, 0.0, above)
    lower = jnp.where(first_is_zero, below, 0.0)
    wide = lane_ids(BLOCK)
    column = lax.rem(wide, W)
    half_lanes = lane_ids(HALF) < CELLS

    def set_halo(halo):
        for b in range(3):
            moved = halo
            if b != 1:
                edge = 0 if b == 0 else W - 1
                moved = jnp.where(column == edge, 0.0, pltpu.roll(halo, (1 - b) % LANES, 1))
            for a in (0, 2):
                halo_ref[3 * a + b] = moved if a == 0 else pltpu.roll(moved, CELLS, 1)

    own_halo[...] = jnp.transpose(
        square_of(jnp.concatenate([upper, zero_rows, lower], axis=0))
    )[:BLOCK]

    for load in loads[7:]:
        load.wait()

    half = TDIM // 2
    lanes = lax.broadcasted_iota(jnp.int32, (8, TDIM), 1)
    index = jnp.where(lanes < half, lanes, lanes - half).astype(F32)
    angles = time_ref[0].astype(F32) * jnp.exp(index * (-math.log(10000.0) / half))
    emb = jnp.where(lanes < half, jnp.cos(angles), jnp.sin(angles))
    semb = (emb / (1.0 + jnp.exp(-emb))).astype(BF16).astype(F32)
    temb = jnp.sum(proj_ref[...].astype(F32) * semb[:1], axis=1, keepdims=True)
    own_packed[2] = pack_column(as_column(bias_ref[...]) + temb)

    def turn():
        for j in range(C // PIECE):
            turned_ref[pl.ds(PIECE * j, PIECE), :] = jnp.transpose(
                weight_ref[:, :, pl.ds(PIECE * j, PIECE)].reshape(TAPS, PIECE)
            )

    @pl.when(jnp.logical_not(swapped))
    def _():
        packed_ref[...] = own_packed[...]
        set_halo(own_halo[...])
        weight_copy.wait()
        turn()

    def remote(src, dst, send, recv, device):
        return pltpu.make_async_remote_copy(
            src_ref=src,
            dst_ref=dst,
            send_sem=send,
            recv_sem=recv,
            device_id=device,
            device_id_type=MESH,
        )

    def block_copy(q, i):
        return remote(
            send_ref.at[q, i],
            recv_ref.at[kind, q, i],
            send_sem.at[q, i],
            recv_sem.at[kind, q, i],
            (target(lax.rem(c + step_of(i), Z)), lax.rem(c + step_of(i), Z), r),
        )

    def base_copy(q):
        return remote(
            base_out_ref.at[q],
            base_ref.at[kind, q],
            base_out_sem.at[q],
            base_sem.at[kind, q],
            (target(c), c, r),
        )

    def back_copy(q):
        return remote(
            back_out_ref.at[q],
            back_ref.at[q],
            back_out_sem.at[q],
            back_sem.at[q],
            (behind, c, r),
        )

    def gathered(which, q, total, between=None):
        for i in range(Z - 2, -1, -1):
            if between is not None and i == PAUSE:
                between()
            slot = recv_ref.at[which, q, i]
            pltpu.make_async_copy(slot, slot, recv_sem.at[which, q, i]).wait()
            total = total + recv_ref[which, q, i].astype(F32)
        return total.astype(BF16)

    def group_mean(rows):
        summed = jnp.sum(rows, axis=0, keepdims=True)
        mask = half_lanes[:1]
        left = jnp.sum(jnp.where(mask, summed, 0.0), axis=1, keepdims=True)
        right = jnp.sum(jnp.where(mask, 0.0, summed), axis=1, keepdims=True)
        return jnp.where(mask, left, right) * (1.0 / (HALF * CELLS))

    def taps_of(q, x):
        mean = group_mean(x)
        centred = x - mean
        variance = group_mean(centred * centred)
        scaled = centred * (1.0 / jnp.sqrt(variance + 1e-05)) * packed_ref[0] + packed_ref[1]
        hidden = scaled / (1.0 + jnp.exp(-scaled))
        taps = []
        for a in range(3):
            for b in range(3):
                shift = W * (a - 1) + b - 1
                moved = jnp.concatenate(
                    [
                        pltpu.roll(hidden, -shift % LANES, 1) if shift else hidden,
                        pltpu.roll(hidden, (CELLS - shift) % LANES, 1),
                    ],
                    axis=0,
                )
                valid = None
                if a != 1:
                    valid = wide >= W if a == 0 else wide < W
                if b != 1:
                    inside = column != (0 if b == 0 else W - 1)
                    valid = inside if valid is None else valid & inside
                if valid is not None:
                    moved = jnp.where(valid, moved, 0.0 if a == 1 else halo_ref[3 * a + b])
                taps.append(moved.astype(BF16))
        return hidden, jnp.concatenate(taps, axis=0)

    def next_halo(hidden):
        spread = jnp.concatenate([pltpu.roll(hidden, W, 1), pltpu.roll(hidden, 3 * W, 1)], axis=0)
        turned_row = pltpu.roll(spread, CELLS, 1)
        set_halo(
            jnp.where(
                first_is_zero,
                jnp.where(wide < W, turned_row, 0.0),
                jnp.where(wide >= 3 * W, turned_row, 0.0),
            )
        )

    def multiply(q, taps, chunk):
        rows = []
        for i in chunk:
            z = c if i == OWN else lax.rem(c + step_of(i), Z)
            rows.append(turned_ref[pl.ds(pl.multiple_of(z * BLOCK, 16), BLOCK), :])
        product = jnp.dot(jnp.concatenate(rows, axis=0), taps, preferred_element_type=F32)
        parts = [pack(product[k * BLOCK : (k + 1) * BLOCK]) for k in range(len(chunk))]
        for i, part in zip(chunk, parts):
            if i != OWN:
                send_ref[q, i] = part.astype(BF16)
        return parts

    def start(q, chunk):
        for i in chunk:
            block_copy(q, i).start()

    def finish(q):

        @pl.when(role < 4)
        def _():
            for i in range(FAR):
                block_copy(q, i).wait_send()

        start(q, NEAR_CHUNK)

    @pl.when(is_first)
    def _():
        for q in range(2):
            x = x_ref[q]
            hidden, taps = taps_of(q, x)
            for chunk in FAR_CHUNKS + MIDDLE_CHUNKS + (NEAR_CHUNK,):
                multiply(q, taps, chunk)
            base_out_ref[q] = x + multiply(q, taps, (OWN,))[0] + packed_ref[2]
            if q == 0:
                next_halo(hidden)

    greeted = jnp.where(stays, Z - 1, Z) + jnp.where(role > 0, 1, 0)
    greeted = greeted + jnp.where(swapped, jnp.where(core == 0, 5, 4), 0)
    pl.semaphore_wait(barrier, greeted)

    @pl.when(swapped)
    def _():
        moves = [
            remote(src, dst, move_out_sem.at[i], move_sem.at[i], (host, c, r))
            for i, (src, dst) in enumerate(
                (
                    (weight_hbm.at[2 * r], weight_ref.at[2 * r]),
                    (weight_hbm.at[2 * r + 1], weight_ref.at[2 * r + 1]),
                    (weight_hbm.at[8], weight_ref.at[8]),
                    (own_packed, packed_ref),
                    (own_halo, given_halo),
                )
            )
        ]

        @pl.when(core == 1)
        def _():
            pl.semaphore_wait(turn_sem, 1)

        for copy in moves:
            copy.start()

        def passed(i, j):
            return remote(
                weight_ref.at[2 * r + j],
                weight_ref.at[2 * r + j],
                pass_out_sem.at[i - 1, j],
                pass_sem.at[i - 1, j],
                (s, c, lax.rem(r + i, 4)),
            )

        for j in range(2):
            moves[j].wait_recv()
            for i in (2, 1, 3):
                passed(i, j).start()
        for copy in moves:
            copy.wait_send()

        @pl.when(core == 0)
        def _():
            pl.semaphore_signal(turn_sem, inc=1, device_id=(s + 1, c, r), device_id_type=MESH)

        for copy in moves[2:]:
            copy.wait_recv()
        set_halo(given_halo[...])
        for j in range(2):
            for i in range(1, 4):
                passed(i, j).wait_send()
                slot = weight_ref.at[2 * lax.rem(r + 4 - i, 4) + j]
                pltpu.make_async_copy(slot, slot, pass_sem.at[i - 1, j]).wait()
        turn()

    @pl.when(is_first)
    def _():
        for q in range(2):
            for chunk in FAR_CHUNKS + MIDDLE_CHUNKS:
                start(q, chunk)
            base_copy(q).start()
            finish(q)

    @pl.when(s > 0)
    def _():
        for q in range(2):
            base = base_ref.at[0, q]
            pltpu.make_async_copy(base, base, base_sem.at[0, q]).wait()
            near = functools.partial(start, 0, NEAR_CHUNK) if q else None
            x = gathered(0, q, base_ref[0, q], near).astype(F32)
            hidden, taps = taps_of(q, x)
            for chunk in FAR_CHUNKS:
                multiply(q, taps, chunk)
                start(q, chunk)
            own = multiply(q, taps, MIDDLE_CHUNKS[0] + MIDDLE_CHUNKS[1] + NEAR_CHUNK + (OWN,))[-1]
            start(q, MIDDLE_CHUNKS[0])
            base_out_ref[q] = x + own + packed_ref[2]

            @pl.when(jnp.logical_not(stays))
            def _():
                base_copy(q).start()

            start(q, MIDDLE_CHUNKS[1])
            back_out_ref[q] = x.astype(BF16)
            back_copy(q).start()
            if q == 0:
                next_halo(hidden)
            else:
                finish(q)

    results = []
    for q in range(2):

        @pl.when(s < last)
        def _():
            back = back_ref.at[q]
            pltpu.make_async_copy(back, back, back_sem.at[q]).wait()
            x_ref[q] = back_ref[q].astype(F32)

        @pl.when(stays)
        def _():
            x_ref[q] = base_out_ref[q]

        @pl.when((s == last) & jnp.logical_not(stays))
        def _():
            base = base_ref.at[1, q]
            pltpu.make_async_copy(base, base, base_sem.at[1, q]).wait()
            x_ref[q] = base_ref[1, q]

        @pl.when(s == last)
        def _():
            x_ref[q] = gathered(1, q, x_ref[q]).astype(F32)

        packed = x_ref[q]
        rows = square_of(jnp.concatenate([packed, pltpu.roll(packed, CELLS, 1)], axis=0))
        results.append(jnp.transpose(rows)[:CELLS, :BLOCK].astype(BF16))
    out_ref[0] = jnp.where(first_is_zero, results[0].astype(F32), results[1].astype(F32)).astype(
        BF16
    )
    out_ref[1] = jnp.where(first_is_zero, results[1].astype(F32), results[0].astype(F32)).astype(
        BF16
    )

    for q in range(2):
        for i in range(FAR, Z - 1):
            block_copy(q, i).wait_send()
        if q == 1:

            @pl.when(role >= 4)
            def _():
                for i in range(FAR):
                    block_copy(1, i).wait_send()

        if q == 0:

            @pl.when(s > 0)
            def _():
                for i in range(FAR):
                    block_copy(0, i).wait_send()

        @pl.when(jnp.logical_not(stays))
        def _():
            base_copy(q).wait_send()

        @pl.when(s > 0)
        def _():
            back_copy(q).wait_send()


def on_device(
    latent,
    stale_rows,
    conv_weight,
    conv_bias,
    norm_gain,
    norm_shift,
    time_proj,
    patch_order,
    timestep,
    stale_step,
):
    out = pl.pallas_call(
        kernel,
        out_shape=pltpu.VMEM((2, CELLS, BLOCK), BF16),
        in_specs=[pl.BlockSpec(memory_space=pltpu.HBM)] * 10,
        out_specs=pl.BlockSpec(memory_space=pltpu.VMEM),
        scratch_shapes=[
            pltpu.SMEM((2,), jnp.int32),
            pltpu.SMEM((1,), jnp.int32),
            pltpu.SMEM((1, 2), jnp.int32),
            pltpu.VMEM((2, CELLS, BLOCK), BF16),
            pltpu.VMEM((STALE, W, BLOCK), BF16),
            pltpu.VMEM((STALE, W, BLOCK), BF16),
            pltpu.VMEM((1, BLOCK), F32),
            pltpu.VMEM((1, BLOCK), F32),
            pltpu.VMEM((1, BLOCK), F32),
            pltpu.VMEM((BLOCK, TDIM), BF16),
            pltpu.VMEM((9, BLOCK, C), BF16),
            pltpu.VMEM((C, TAPS), BF16),
            pltpu.VMEM((3, HALF, LANES), F32),
            pltpu.VMEM((3, HALF, LANES), F32),
            pltpu.VMEM((BLOCK, LANES), F32),
            pltpu.VMEM((BLOCK, LANES), F32),
            pltpu.VMEM((9, BLOCK, LANES), F32),
            pltpu.VMEM((2, HALF, LANES), F32),
            pltpu.VMEM((2, 2, Z - 1, HALF, LANES), BF16),
            pltpu.VMEM((2, 2, HALF, LANES), F32),
            pltpu.VMEM((2, Z - 1, HALF, LANES), BF16),
            pltpu.VMEM((2, HALF, LANES), F32),
            pltpu.VMEM((2, HALF, LANES), BF16),
            pltpu.VMEM((2, HALF, LANES), BF16),
            pltpu.SemaphoreType.DMA,
            pltpu.SemaphoreType.DMA((10,)),
            pltpu.SemaphoreType.DMA((5,)),
            pltpu.SemaphoreType.DMA((5,)),
            pltpu.SemaphoreType.DMA((3, 2)),
            pltpu.SemaphoreType.DMA((3, 2)),
            pltpu.SemaphoreType.REGULAR,
            pltpu.SemaphoreType.DMA((2, 2, Z - 1)),
            pltpu.SemaphoreType.DMA((2, 2)),
            pltpu.SemaphoreType.DMA((2, Z - 1)),
            pltpu.SemaphoreType.DMA((2,)),
            pltpu.SemaphoreType.DMA((2,)),
            pltpu.SemaphoreType.DMA((2,)),
        ],
        compiler_params=pltpu.CompilerParams(
            collective_id=0, has_side_effects=True, vmem_limit_bytes=60 * 1024 * 1024
        ),
        name="segments",
    )(
        patch_order,
        timestep,
        stale_step,
        jnp.transpose(latent, (0, 2, 1)),
        jnp.transpose(stale_rows[:, 0], (0, 1, 3, 4, 2)),
        conv_weight[0],
        conv_bias,
        norm_gain,
        norm_shift,
        jnp.transpose(time_proj[0]),
    )
    return jnp.transpose(out, (0, 2, 1))[None]


def solution(mesh):
    placed = (
        P("rep", "chan", None),
        P(None, "section", "rep", "chan", None, None),
        P("section", None, "chan", None),
        P("section", "chan"),
        P("section", "chan"),
        P("section", "chan"),
        P("section", None, "chan"),
        P(),
        P("rep"),
        P("section", None),
    )
    return jax.shard_map(
        on_device,
        mesh=mesh,
        in_specs=placed,
        out_specs=P("section", "rep", "chan", None),
        check_vma=False,
    )
```

```python
import functools
import math

import jax
import jax.numpy as jnp
from jax import lax
from jax.experimental import pallas as pl
from jax.experimental.pallas import tpu as pltpu
from jax.sharding import PartitionSpec as P

C = 1280
TDIM = 320
W = 32
CELLS = 64
STALE = 4
SECTIONS = 8
Z = 16
BLOCK = 80
HALF = 40
PIECE = 256
TAPS = 9 * BLOCK
LANES = 128
OWN = Z - 1
FAR_CHUNKS = ((0,), (1, 2), (3, 4, 5, 6))
MIDDLE_CHUNKS = ((7, 8), (9, 10))
NEAR_CHUNK = (11, 12, 13, 14)
FAR = 7
PAUSE = 6
MESH = pl.DeviceIdType.MESH
F32 = jnp.float32
BF16 = jnp.bfloat16


def step_of(i):
    if i == 0:
        return Z // 2
    distance = Z // 2 - (i + 1) // 2
    return distance if i % 2 else Z - distance


def odd(z):
    return lax.rem(z, 2) == 1


def holder(t, z):
    moved = jnp.where(t < 6, t + 2, t - 2)
    return jnp.where(odd(z) & (t >= 4), moved, t)


def section_of(s, z):
    taken = jnp.where(s < 6, s + 2, s - 2)
    return jnp.where(odd(z) & (s >= 4), taken, s)


def lane_ids(rows):
    return lax.broadcasted_iota(jnp.int32, (rows, LANES), 1)


def as_column(row):
    square = jnp.broadcast_to(row, (BLOCK, BLOCK))
    diagonal = lax.broadcasted_iota(jnp.int32, (BLOCK, BLOCK), 0) == lax.broadcasted_iota(
        jnp.int32, (BLOCK, BLOCK), 1
    )
    return jnp.sum(jnp.where(diagonal, square, 0.0), axis=1, keepdims=True)


def pack_column(column):
    left = jnp.broadcast_to(column[:HALF], (HALF, LANES))
    right = jnp.broadcast_to(column[HALF:], (HALF, LANES))
    return jnp.where(lane_ids(HALF) < CELLS, left, right)


def pack(block):
    return jnp.where(lane_ids(HALF) < CELLS, block[:HALF], pltpu.roll(block[HALF:], CELLS, 1))


def square_of(rows):
    short_lanes = LANES - rows.shape[1]
    if short_lanes:
        rows = jnp.concatenate([rows, jnp.zeros((rows.shape[0], short_lanes), F32)], axis=1)
    short = LANES - rows.shape[0]
    if short:
        rows = jnp.concatenate([rows, jnp.zeros((short, LANES), F32)], axis=0)
    return rows


def kernel(
    order_hbm,
    time_hbm,
    step_hbm,
    latent_hbm,
    stale_hbm,
    weight_hbm,
    bias_hbm,
    gain_hbm,
    shift_hbm,
    proj_hbm,
    out_ref,
    order_ref,
    time_ref,
    step_ref,
    latent_ref,
    below_ref,
    above_ref,
    bias_ref,
    gain_ref,
    shift_ref,
    proj_ref,
    weight_ref,
    turned_ref,
    own_packed,
    packed_ref,
    own_halo,
    given_halo,
    halo_ref,
    x_ref,
    recv_ref,
    base_ref,
    send_ref,
    base_out_ref,
    back_ref,
    back_out_ref,
    weight_sem,
    load_sem,
    move_out_sem,
    move_sem,
    pass_out_sem,
    pass_sem,
    turn_sem,
    recv_sem,
    base_sem,
    send_sem,
    base_out_sem,
    back_sem,
    back_out_sem,
):
    s = lax.axis_index("section")
    c = lax.axis_index("chan")
    r = lax.axis_index("rep")
    last = SECTIONS - 1
    is_first = s == 0
    role = section_of(s, c)
    host = holder(s, c)
    swapped = role != s
    core = lax.rem(s, 2)
    ends = role == last
    stays = ends & (s == last)
    kind = jnp.where(ends, 1, 0)
    ahead = jnp.minimum(role + 1, last)
    behind = jnp.maximum(role - 1, 0)

    def target(z):
        return jnp.where(ends, last, holder(ahead, z))

    loads = [
        pltpu.make_async_copy(src, dst, load_sem.at[i])
        for i, (src, dst) in enumerate(
            (
                (latent_hbm, latent_ref),
                (order_hbm, order_ref),
                (gain_hbm, gain_ref),
                (shift_hbm, shift_ref),
                (step_hbm, step_ref),
                (stale_hbm.at[:, 1, 0], below_ref),
                (stale_hbm.at[:, 0, 1], above_ref),
                (time_hbm, time_ref),
                (bias_hbm, bias_ref),
                (proj_hbm, proj_ref),
            )
        )
    ]
    weight_copy = pltpu.make_async_copy(weight_hbm, weight_ref, weight_sem)

    def greet(section, z):
        pl.semaphore_signal(barrier, inc=1, device_id=(section, z, r), device_id_type=MESH)

    barrier = pltpu.get_barrier_semaphore()

    @pl.when(role > 0)
    def _():
        for i in range(Z):
            z = lax.rem(c + step_of(i), Z) if i < OWN else c
            greet(holder(behind, z), z)

    @pl.when(s == last)
    def _():
        for i in range(Z - 1):
            z = lax.rem(c + step_of(i), Z)
            greet(holder(last, z), z)

    @pl.when((s == last) & swapped)
    def _():
        greet(holder(last, c), c)

    @pl.when(s < last)
    def _():
        greet(holder(s + 1, c), c)

    @pl.when(swapped)
    def _():
        greet(role, c)
        for i in range(1, 4):
            pl.semaphore_signal(
                barrier, inc=1, device_id=(s, c, lax.rem(r + i, 4)), device_id_type=MESH
            )

    @pl.when(swapped & (core == 1))
    def _():
        greet(s - 1, c)

    for load in loads[:7]:
        load.start()

    @pl.when(jnp.logical_not(swapped))
    def _():
        weight_copy.start()

    for load in loads[7:]:
        load.start()

    for load in loads[:7]:
        load.wait()
    first_is_zero = order_ref[0] == 0

    own_packed[0] = pack_column(as_column(gain_ref[...]))
    own_packed[1] = pack_column(as_column(shift_ref[...]))

    @pl.when(is_first)
    def _():
        packed = [pack(jnp.transpose(square_of(latent_ref[p].astype(F32)))[:BLOCK]) for p in (0, 1)]
        x_ref[0] = jnp.where(first_is_zero, packed[0], packed[1])
        x_ref[1] = jnp.where(first_is_zero, packed[1], packed[0])

    below = jnp.zeros((W, BLOCK), F32)
    above = jnp.zeros((W, BLOCK), F32)
    for k in range(STALE):
        below = below + jnp.where(step_ref[0, 1] == k, below_ref[k].astype(F32), 0.0)
        above = above + jnp.where(step_ref[0, 0] == k, above_ref[k].astype(F32), 0.0)
    zero_rows = jnp.zeros((2 * W, BLOCK), F32)
    upper = jnp.where(first_is_zero, 0.0, above)
    lower = jnp.where(first_is_zero, below, 0.0)
    wide = lane_ids(BLOCK)
    column = lax.rem(wide, W)
    half_lanes = lane_ids(HALF) < CELLS

    def set_halo(halo):
        for b in range(3):
            moved = halo
            if b != 1:
                edge = 0 if b == 0 else W - 1
                moved = jnp.where(column == edge, 0.0, pltpu.roll(halo, (1 - b) % LANES, 1))
            for a in (0, 2):
                halo_ref[3 * a + b] = moved if a == 0 else pltpu.roll(moved, CELLS, 1)

    own_halo[...] = jnp.transpose(
        square_of(jnp.concatenate([upper, zero_rows, lower], axis=0))
    )[:BLOCK]

    for load in loads[7:]:
        load.wait()

    half = TDIM // 2
    lanes = lax.broadcasted_iota(jnp.int32, (8, TDIM), 1)
    index = jnp.where(lanes < half, lanes, lanes - half).astype(F32)
    angles = time_ref[0].astype(F32) * jnp.exp(index * (-math.log(10000.0) / half))
    emb = jnp.where(lanes < half, jnp.cos(angles), jnp.sin(angles))
    semb = (emb / (1.0 + jnp.exp(-emb))).astype(BF16).astype(F32)
    temb = jnp.sum(proj_ref[...].astype(F32) * semb[:1], axis=1, keepdims=True)
    own_packed[2] = pack_column(as_column(bias_ref[...]) + temb)

    def turn():
        for j in range(C // PIECE):
            turned_ref[pl.ds(PIECE * j, PIECE), :] = jnp.transpose(
                weight_ref[:, :, pl.ds(PIECE * j, PIECE)].reshape(TAPS, PIECE)
            )

    @pl.when(jnp.logical_not(swapped))
    def _():
        packed_ref[...] = own_packed[...]
        set_halo(own_halo[...])
        weight_copy.wait()
        turn()

    def remote(src, dst, send, recv, device):
        return pltpu.make_async_remote_copy(
            src_ref=src,
            dst_ref=dst,
            send_sem=send,
            recv_sem=recv,
            device_id=device,
            device_id_type=MESH,
        )

    def block_copy(q, i):
        return remote(
            send_ref.at[q, i],
            recv_ref.at[kind, q, i],
            send_sem.at[q, i],
            recv_sem.at[kind, q, i],
            (target(lax.rem(c + step_of(i), Z)), lax.rem(c + step_of(i), Z), r),
        )

    def base_copy(q):
        return remote(
            base_out_ref.at[q],
            base_ref.at[kind, q],
            base_out_sem.at[q],
            base_sem.at[kind, q],
            (target(c), c, r),
        )

    def back_copy(q):
        return remote(
            back_out_ref.at[q],
            back_ref.at[q],
            back_out_sem.at[q],
            back_sem.at[q],
            (behind, c, r),
        )

    def gathered(which, q, total, between=None):
        for i in range(Z - 2, -1, -1):
            if between is not None and i == PAUSE:
                between()
            slot = recv_ref.at[which, q, i]
            pltpu.make_async_copy(slot, slot, recv_sem.at[which, q, i]).wait()
            total = total + recv_ref[which, q, i].astype(F32)
        return total.astype(BF16)

    def group_mean(rows):
        summed = jnp.sum(rows, axis=0, keepdims=True)
        mask = half_lanes[:1]
        left = jnp.sum(jnp.where(mask, summed, 0.0), axis=1, keepdims=True)
        right = jnp.sum(jnp.where(mask, 0.0, summed), axis=1, keepdims=True)
        return jnp.where(mask, left, right) * (1.0 / (HALF * CELLS))

    def taps_of(q, x):
        mean = group_mean(x)
        centred = x - mean
        variance = group_mean(centred * centred)
        scaled = centred * (1.0 / jnp.sqrt(variance + 1e-05)) * packed_ref[0] + packed_ref[1]
        hidden = scaled / (1.0 + jnp.exp(-scaled))
        taps = []
        for a in range(3):
            for b in range(3):
                shift = W * (a - 1) + b - 1
                moved = jnp.concatenate(
                    [
                        pltpu.roll(hidden, -shift % LANES, 1) if shift else hidden,
                        pltpu.roll(hidden, (CELLS - shift) % LANES, 1),
                    ],
                    axis=0,
                )
                valid = None
                if a != 1:
                    valid = wide >= W if a == 0 else wide < W
                if b != 1:
                    inside = column != (0 if b == 0 else W - 1)
                    valid = inside if valid is None else valid & inside
                if valid is not None:
                    moved = jnp.where(valid, moved, 0.0 if a == 1 else halo_ref[3 * a + b])
                taps.append(moved.astype(BF16))
        return hidden, jnp.concatenate(taps, axis=0)

    def next_halo(hidden):
        spread = jnp.concatenate([pltpu.roll(hidden, W, 1), pltpu.roll(hidden, 3 * W, 1)], axis=0)
        turned_row = pltpu.roll(spread, CELLS, 1)
        set_halo(
            jnp.where(
                first_is_zero,
                jnp.where(wide < W, turned_row, 0.0),
                jnp.where(wide >= 3 * W, turned_row, 0.0),
            )
        )

    def multiply(q, taps, chunk):
        rows = []
        for i in chunk:
            z = c if i == OWN else lax.rem(c + step_of(i), Z)
            rows.append(turned_ref[pl.ds(pl.multiple_of(z * BLOCK, 16), BLOCK), :])
        product = jnp.dot(jnp.concatenate(rows, axis=0), taps, preferred_element_type=F32)
        parts = [pack(product[k * BLOCK : (k + 1) * BLOCK]) for k in range(len(chunk))]
        for i, part in zip(chunk, parts):
            if i != OWN:
                send_ref[q, i] = part.astype(BF16)
        return parts

    def start(q, chunk):
        for i in chunk:
            block_copy(q, i).start()

    def finish(q):

        @pl.when(role < 3)
        def _():
            for i in range(FAR):
                block_copy(q, i).wait_send()

        start(q, NEAR_CHUNK)

    @pl.when(is_first)
    def _():
        for q in range(2):
            x = x_ref[q]
            hidden, taps = taps_of(q, x)
            for chunk in FAR_CHUNKS + MIDDLE_CHUNKS + (NEAR_CHUNK,):
                multiply(q, taps, chunk)
            base_out_ref[q] = x + multiply(q, taps, (OWN,))[0] + packed_ref[2]
            if q == 0:
                next_halo(hidden)

    greeted = jnp.where(stays, Z - 1, Z) + jnp.where(role > 0, 1, 0)
    greeted = greeted + jnp.where(swapped, jnp.where(core == 0, 5, 4), 0)
    pl.semaphore_wait(barrier, greeted)

    @pl.when(swapped)
    def _():
        moves = [
            remote(src, dst, move_out_sem.at[i], move_sem.at[i], (host, c, r))
            for i, (src, dst) in enumerate(
                (
                    (weight_hbm.at[2 * r], weight_ref.at[2 * r]),
                    (weight_hbm.at[2 * r + 1], weight_ref.at[2 * r + 1]),
                    (weight_hbm.at[8], weight_ref.at[8]),
                    (own_packed, packed_ref),
                    (own_halo, given_halo),
                )
            )
        ]

        @pl.when(core == 1)
        def _():
            pl.semaphore_wait(turn_sem, 1)

        for copy in moves:
            copy.start()

        def passed(i, j):
            return remote(
                weight_ref.at[2 * r + j],
                weight_ref.at[2 * r + j],
                pass_out_sem.at[i - 1, j],
                pass_sem.at[i - 1, j],
                (s, c, lax.rem(r + i, 4)),
            )

        for j in range(2):
            moves[j].wait_recv()
            for i in (2, 1, 3):
                passed(i, j).start()
        for copy in moves:
            copy.wait_send()

        @pl.when(core == 0)
        def _():
            pl.semaphore_signal(turn_sem, inc=1, device_id=(s + 1, c, r), device_id_type=MESH)

        for copy in moves[2:]:
            copy.wait_recv()
        set_halo(given_halo[...])
        for j in range(2):
            for i in range(1, 4):
                passed(i, j).wait_send()
                slot = weight_ref.at[2 * lax.rem(r + 4 - i, 4) + j]
                pltpu.make_async_copy(slot, slot, pass_sem.at[i - 1, j]).wait()
        turn()

    @pl.when(is_first)
    def _():
        for q in range(2):
            for chunk in FAR_CHUNKS + MIDDLE_CHUNKS:
                start(q, chunk)
            base_copy(q).start()
            finish(q)

    @pl.when(s > 0)
    def _():
        for q in range(2):
            base = base_ref.at[0, q]
            pltpu.make_async_copy(base, base, base_sem.at[0, q]).wait()
            near = functools.partial(start, 0, NEAR_CHUNK) if q else None
            x = gathered(0, q, base_ref[0, q], near).astype(F32)
            hidden, taps = taps_of(q, x)
            for chunk in FAR_CHUNKS:
                multiply(q, taps, chunk)
                start(q, chunk)
            own = multiply(q, taps, MIDDLE_CHUNKS[0] + MIDDLE_CHUNKS[1] + NEAR_CHUNK + (OWN,))[-1]
            start(q, MIDDLE_CHUNKS[0])
            base_out_ref[q] = x + own + packed_ref[2]

            @pl.when(jnp.logical_not(stays))
            def _():
                base_copy(q).start()

            start(q, MIDDLE_CHUNKS[1])
            back_out_ref[q] = x.astype(BF16)
            back_copy(q).start()
            if q == 0:
                next_halo(hidden)
            else:
                finish(q)

    results = []
    for q in range(2):

        @pl.when(s < last)
        def _():
            back = back_ref.at[q]
            pltpu.make_async_copy(back, back, back_sem.at[q]).wait()
            x_ref[q] = back_ref[q].astype(F32)

        @pl.when(stays)
        def _():
            x_ref[q] = base_out_ref[q]

        @pl.when((s == last) & jnp.logical_not(stays))
        def _():
            base = base_ref.at[1, q]
            pltpu.make_async_copy(base, base, base_sem.at[1, q]).wait()
            x_ref[q] = base_ref[1, q]

        @pl.when(s == last)
        def _():
            x_ref[q] = gathered(1, q, x_ref[q]).astype(F32)

        packed = x_ref[q]
        rows = square_of(jnp.concatenate([packed, pltpu.roll(packed, CELLS, 1)], axis=0))
        results.append(jnp.transpose(rows)[:CELLS, :BLOCK].astype(BF16))
    out_ref[0] = jnp.where(first_is_zero, results[0].astype(F32), results[1].astype(F32)).astype(
        BF16
    )
    out_ref[1] = jnp.where(first_is_zero, results[1].astype(F32), results[0].astype(F32)).astype(
        BF16
    )

    for q in range(2):
        for i in range(FAR, Z - 1):
            block_copy(q, i).wait_send()
        if q == 1:

            @pl.when(role >= 3)
            def _():
                for i in range(FAR):
                    block_copy(1, i).wait_send()

        if q == 0:

            @pl.when(s > 0)
            def _():
                for i in range(FAR):
                    block_copy(0, i).wait_send()

        @pl.when(jnp.logical_not(stays))
        def _():
            base_copy(q).wait_send()

        @pl.when(s > 0)
        def _():
            back_copy(q).wait_send()


def on_device(
    latent,
    stale_rows,
    conv_weight,
    conv_bias,
    norm_gain,
    norm_shift,
    time_proj,
    patch_order,
    timestep,
    stale_step,
):
    out = pl.pallas_call(
        kernel,
        out_shape=pltpu.VMEM((2, CELLS, BLOCK), BF16),
        in_specs=[pl.BlockSpec(memory_space=pltpu.HBM)] * 10,
        out_specs=pl.BlockSpec(memory_space=pltpu.VMEM),
        scratch_shapes=[
            pltpu.SMEM((2,), jnp.int32),
            pltpu.SMEM((1,), jnp.int32),
            pltpu.SMEM((1, 2), jnp.int32),
            pltpu.VMEM((2, CELLS, BLOCK), BF16),
            pltpu.VMEM((STALE, W, BLOCK), BF16),
            pltpu.VMEM((STALE, W, BLOCK), BF16),
            pltpu.VMEM((1, BLOCK), F32),
            pltpu.VMEM((1, BLOCK), F32),
            pltpu.VMEM((1, BLOCK), F32),
            pltpu.VMEM((BLOCK, TDIM), BF16),
            pltpu.VMEM((9, BLOCK, C), BF16),
            pltpu.VMEM((C, TAPS), BF16),
            pltpu.VMEM((3, HALF, LANES), F32),
            pltpu.VMEM((3, HALF, LANES), F32),
            pltpu.VMEM((BLOCK, LANES), F32),
            pltpu.VMEM((BLOCK, LANES), F32),
            pltpu.VMEM((9, BLOCK, LANES), F32),
            pltpu.VMEM((2, HALF, LANES), F32),
            pltpu.VMEM((2, 2, Z - 1, HALF, LANES), BF16),
            pltpu.VMEM((2, 2, HALF, LANES), F32),
            pltpu.VMEM((2, Z - 1, HALF, LANES), BF16),
            pltpu.VMEM((2, HALF, LANES), F32),
            pltpu.VMEM((2, HALF, LANES), BF16),
            pltpu.VMEM((2, HALF, LANES), BF16),
            pltpu.SemaphoreType.DMA,
            pltpu.SemaphoreType.DMA((10,)),
            pltpu.SemaphoreType.DMA((5,)),
            pltpu.SemaphoreType.DMA((5,)),
            pltpu.SemaphoreType.DMA((3, 2)),
            pltpu.SemaphoreType.DMA((3, 2)),
            pltpu.SemaphoreType.REGULAR,
            pltpu.SemaphoreType.DMA((2, 2, Z - 1)),
            pltpu.SemaphoreType.DMA((2, 2)),
            pltpu.SemaphoreType.DMA((2, Z - 1)),
            pltpu.SemaphoreType.DMA((2,)),
            pltpu.SemaphoreType.DMA((2,)),
            pltpu.SemaphoreType.DMA((2,)),
        ],
        compiler_params=pltpu.CompilerParams(
            collective_id=0, has_side_effects=True, vmem_limit_bytes=60 * 1024 * 1024
        ),
        name="segments",
    )(
        patch_order,
        timestep,
        stale_step,
        jnp.transpose(latent, (0, 2, 1)),
        jnp.transpose(stale_rows[:, 0], (0, 1, 3, 4, 2)),
        conv_weight[0],
        conv_bias,
        norm_gain,
        norm_shift,
        jnp.transpose(time_proj[0]),
    )
    return jnp.transpose(out, (0, 2, 1))[None]


def solution(mesh):
    placed = (
        P("rep", "chan", None),
        P(None, "section", "rep", "chan", None, None),
        P("section", None, "chan", None),
        P("section", "chan"),
        P("section", "chan"),
        P("section", "chan"),
        P("section", None, "chan"),
        P(),
        P("rep"),
        P("section", None),
    )
    return jax.shard_map(
        on_device,
        mesh=mesh,
        in_specs=placed,
        out_specs=P("section", "rep", "chan", None),
        check_vma=False,
    )
```
